256 devices in a mesh: shot: 8 (over z_hi, y), pencil: 32 (over z_lo, x, core).
Axes of the slice: x: 4, y: 4, z: 8 (z_hi: 2, z_lo: 4; z = z_hi * 4 + z_lo), core: 2. Of those that a mesh axis runs over, the one named last changes fastest.
Arguments:
- contrast_source: float32 [16, 2, 256, 256, 128], P('shot', None, 'pencil'), may hold values from -6 to 6
- green_spectrum: float32 [2, 256, 256, 128], P(None, None, 'pencil'), may hold values from -4 to 4
- source_cells: int32 [16, 3], P('shot'), may hold values from 0 to 127
Outputs:
- updated_source: float32 [16, 2, 256, 256, 128], P('shot', None, 'pencil')
- contrast: float32 [2, 256, 256, 128], P(None, 'pencil', 'shot')
The draws below stay inside these ranges and needn't reach their ends.
Inputs may be any that keep to these rules, and one draw needn't show every extreme that they name: `source_cells`: each row is one source's cell (x, y, z).
All inputs are finite; a program needn't handle non-finite values.
Results may differ from the reference program's by a relative error of at most 0.0003.
Values sent between devices are 32-bit elements; how exact they have to be, the bound alone decides.
No kernel may reach another device: no remote copies, remote signals or barrier semaphores. Data moves between devices by JAX's collectives and lax.ppermute only.
A program may use at most 64 MiB of HBM per device.

```python
import math
import jax
import jax.numpy as jnp
from jax import lax

NX = 256
NY = 256
NZ = 128
SOURCES = 16


def set_ends(entries, stream_key, smallest, high):
    index_at = [jax.random.randint(jax.random.fold_in(stream_key, axis), (), 0, length) for axis, length in enumerate(entries.shape)]
    longest = entries.shape.index(max(entries.shape))
    neighbour = index_at[:longest] + [(index_at[longest] + 1) % entries.shape[longest]] + index_at[longest + 1:]
    return entries.at[tuple(index_at)].set(smallest).at[tuple(neighbour)].set(high)


def steps_of(stream_key, extent, pieces, smallest, high):
    def one(position, shards_of):
        steps = jax.random.uniform(jax.random.fold_in(jax.random.fold_in(stream_key, 6), position), (shards_of,), jnp.float32, smallest / len(pieces), high / len(pieces))
        return jnp.repeat(jnp.exp(steps), extent[position] // shards_of).reshape((-1,) + (1,) * (len(extent) - position - 1))

    level = one(*pieces[0])
    for cut in pieces[1:]:
        level = level * one(*cut)
    return level


def normal_values(stream_key, shape, deviation, most, split=(), kind=jnp.bfloat16):
    values = jax.random.normal(stream_key, shape, jnp.float32) * deviation
    if len(split) > 0:
        values = steps_of(stream_key, shape, split, -0.22, 0.18) * values
    return jnp.clip(values, min=-most, max=most).astype(kind)


def setup_inputs(seed: int = 0) -> dict:
    seeds = jax.random.split(jax.random.key(seed), 4)
    contrast_source = normal_values(seeds[0], (SOURCES, 2, NX, NY, NZ), 1.0, 6.0, ((0, 8), (2, 32)), jnp.float32)
    green_spectrum = normal_values(seeds[1], (2, NX, NY, NZ), 0.6, 4.0, ((2, 32),), jnp.float32)
    source_cells = set_ends(jax.random.randint(seeds[2], (SOURCES, 3), 0, NZ), jax.random.fold_in(seeds[2], 1), 0, NZ - 1).astype(jnp.int32)
    return {"contrast_source": contrast_source, "green_spectrum": green_spectrum, "source_cells": source_cells}


def phase_spectrum(cells):
    wave_x = jnp.arange(NX, dtype=jnp.int32)
    wave_y = jnp.arange(NY, dtype=jnp.int32)
    wave_z = jnp.arange(NZ, dtype=jnp.int32)
    turns = ((wave_x * cells[0]) % NX).astype(jnp.float32)[:, None, None] / NX
    turns = turns + ((wave_y * cells[1]) % NY).astype(jnp.float32)[None, :, None] / NY
    turns = turns + ((wave_z * cells[2]) % NZ).astype(jnp.float32)[None, None, :] / NZ
    angle = 2.0 * math.pi * turns
    return jnp.cos(angle), jnp.sin(angle)


def total_field(source, cells, green):
    spectra = jnp.fft.fftn(lax.complex(source[0], source[1]), norm="ortho")
    cosine, sine = phase_spectrum(cells)
    spectra = spectra + lax.complex(cosine, -sine)
    field_of = jnp.fft.ifftn(green * spectra, norm="ortho")
    return jnp.real(field_of), jnp.imag(field_of)


def reference(contrast_source, green_spectrum, source_cells):
    green = lax.complex(green_spectrum[0], green_spectrum[1])
    zeros_grid = jnp.zeros((NX, NY, NZ), jnp.float32)

    def accumulate(carry, item):
        source, cells = item
        field_re, field_im = total_field(source, cells, green)
        numer_re, numer_im, weight = carry
        numer_re = numer_re + field_re * source[0] + field_im * source[1]
        numer_im = numer_im + field_re * source[1] - field_im * source[0]
        weight = weight + field_re * field_re + field_im * field_im
        return (numer_re, numer_im, weight), None

    (numer_re, numer_im, weight), _ = lax.scan(accumulate, (zeros_grid, zeros_grid, zeros_grid), (contrast_source, source_cells))
    contrast_re = numer_re / (1.0 + weight)
    contrast_im = numer_im / (1.0 + weight)

    def update(item):
        source, cells = item
        field_re, field_im = total_field(source, cells, green)
        new_re = 0.5 * (source[0] + contrast_re * field_re - contrast_im * field_im)
        new_im = 0.5 * (source[1] + contrast_re * field_im + contrast_im * field_re)
        return jnp.stack([new_re, new_im])

    updated = lax.map(update, (contrast_source, source_cells))
    return updated, jnp.stack([contrast_re, contrast_im])
```

```python
import functools
import math

import jax
import jax.numpy as jnp
import ml_dtypes
import numpy as np
from jax import lax
from jax.experimental import pallas as pl
from jax.experimental.pallas import tpu as pltpu
from jax.sharding import Mesh, PartitionSpec as P

SHOT = ("zh", "y")
PENCIL = ("zl", "x", "core")
ZH, YY = 2, 4
PARTS = 32
NX, NY, NZ = 256, 256, 128
PLANES = NX // PARTS
KY = NY // PARTS
SHARE = NY // (ZH * YY)
VMEM_LIMIT = 58 * 1024 * 1024


def split_table(table):
    high = table.astype(ml_dtypes.bfloat16)
    return high, (table - high.astype(np.float64)).astype(ml_dtypes.bfloat16)


def cos_sin(length):
    index = np.arange(length)
    angle = 2.0 * np.pi * (index[:, None] * index[None, :] % length) / length
    return np.cos(angle) / math.sqrt(length), np.sin(angle) / math.sqrt(length)


def long_table(order=None):
    cosine, sine = cos_sin(NY)
    if order is not None:
        cosine, sine = cosine[order], sine[order]
    high, low = split_table(np.concatenate([cosine, sine], axis=0))
    return np.concatenate([high, high, low], axis=1)


def z_table(sign):
    cosine, sine = cos_sin(NZ)
    high, low = split_table(np.block([[cosine, -sign * sine], [sign * sine, cosine]]))
    return np.concatenate([high, high, low], axis=0)


def three_terms(values, axis):
    high = values.astype(jnp.bfloat16)
    low = (values - high.astype(jnp.float32)).astype(jnp.bfloat16)
    return jnp.concatenate([high, low, high], axis=axis)


def dot(left, right):
    return lax.dot_general(left, right, (((1,), (0,)), ((), ())), preferred_element_type=jnp.float32)


def long_transform(table, values, sign):
    both = dot(table, three_terms(values, 0))
    count, lanes = both.shape[0] // 2, both.shape[1] // 2
    cos_re, cos_im = both[:count, :lanes], both[:count, lanes:]
    sin_re, sin_im = both[count:, :lanes], both[count:, lanes:]
    if sign > 0:
        return cos_re + sin_im, cos_im - sin_re
    return cos_re - sin_im, cos_im + sin_re


def table_spec(table):
    return pl.BlockSpec(table.shape, lambda *_: (0, 0))


def forward_kernel(member, cell_ref, w_ref, z_ref, y_ref, out_ref):
    plane = lax.axis_index(PENCIL) * PLANES + pl.program_id(0)
    real = w_ref[0, 0, 0]
    imag = w_ref[0, 1, 0]
    row = lax.broadcasted_iota(jnp.int32, (NY, NZ), 0)
    column = lax.broadcasted_iota(jnp.int32, (NY, NZ), 1)
    here = (row == cell_ref[member, 1]) & (column == cell_ref[member, 2])
    here = here & (plane == cell_ref[member, 0])
    real = real + jnp.where(here, math.sqrt(NX * NY * NZ), 0.0)
    values = jnp.concatenate([real, imag], axis=1)
    values = dot(three_terms(values, 1), z_ref[...])
    real, imag = long_transform(y_ref[...], values, 1)
    out_ref[:, 0, 0] = real.reshape(PARTS, KY, NZ)
    out_ref[:, 0, 1] = imag.reshape(PARTS, KY, NZ)


def forward(source, member, cells, z_dft, y_dft):
    return pl.pallas_call(
        functools.partial(forward_kernel, member),
        grid=(PLANES,),
        in_specs=[
            pl.BlockSpec(memory_space=pltpu.SMEM),
            pl.BlockSpec((1, 2, 1, NY, NZ), lambda i: (member, 0, i, 0, 0)),
            *[table_spec(t) for t in (z_dft, y_dft)],
        ],
        out_specs=pl.BlockSpec((PARTS, 1, 2, KY, NZ), lambda i: (0, i, 0, 0, 0)),
        out_shape=jax.ShapeDtypeStruct((PARTS, PLANES, 2, KY, NZ), jnp.float32),
        compiler_params=pltpu.CompilerParams(vmem_limit_bytes=VMEM_LIMIT),
        cost_estimate=pl.CostEstimate(flops=2400 * 10**6, bytes_accessed=4 * 2**20, transcendentals=0),
        name="forward_zy",
    )(cells, source, z_dft, y_dft)


def spectral_kernel(chunks, in_ref, green_ref, x_ref, back_ref, *refs):
    out_refs = [ref.reshape(PARTS * chunk * 2 * KY, NZ) for ref, chunk in zip(refs[-len(chunks) :], chunks)]

    def step(ky, carry):
        def take(c):
            return in_ref[pl.ds(c * KY + ky, NX, stride=2 * KY), :]

        values = jnp.concatenate([take(0), take(1)], axis=1)
        real, imag = long_transform(x_ref[...], values, 1)
        green_re = green_ref[pl.ds(ky, NX, stride=KY), :]
        green_im = green_ref[pl.ds(NX * KY + ky, NX, stride=KY), :]
        values = jnp.concatenate(
            [green_re * real - green_im * imag, green_re * imag + green_im * real], axis=1
        )
        results = long_transform(back_ref[...], values, -1)
        at = 0
        for chunk, out_ref in zip(chunks, out_refs):
            for plane in range(chunk):
                for c in range(2):
                    first = (plane * 2 + c) * KY + ky
                    rows = pl.ds(first, PARTS, stride=chunk * 2 * KY)
                    out_ref[rows, :] = results[c][at : at + PARTS]
                at += PARTS
        return carry

    lax.fori_loop(0, KY, step, 0)


def spectral(spectra, green, member, chunks, x_dft, back_dft, earlier):
    rows = 2 * KY * PARTS
    whole = [(rows * PLANES, NZ), (2 * NX * KY, NZ), *[t.shape for t in (x_dft, back_dft)]]
    return pl.pallas_call(
        functools.partial(spectral_kernel, chunks),
        grid=(1,),
        in_specs=[
            *[pl.BlockSpec(shape, lambda i: (0, 0)) for shape in whole],
            *[pl.BlockSpec(memory_space=pl.ANY) for _ in earlier],
        ],
        out_specs=[
            pl.BlockSpec((PARTS, 1, chunk, 2, KY, NZ), lambda i: (0, member, 0, 0, 0, 0))
            for chunk in chunks
        ],
        out_shape=[
            jax.ShapeDtypeStruct((PARTS, 2, chunk, 2, KY, NZ), jnp.float32) for chunk in chunks
        ],
        input_output_aliases={4 + i: i for i in range(len(earlier))},
        compiler_params=pltpu.CompilerParams(vmem_limit_bytes=VMEM_LIMIT),
        cost_estimate=pl.CostEstimate(flops=3200 * 10**6, bytes_accessed=6 * 2**20, transcendentals=0),
        name="spectral",
    )(
        spectra.reshape(rows * PLANES, NZ),
        green.reshape(2 * NX * KY, NZ),
        x_dft,
        back_dft,
        *earlier,
    )


def inverse_kernel(f_ref, w_ref, z_ref, y_ref, u_ref, sum_ref):
    here = lax.axis_index("y")
    total_re = total_im = weight = None
    for member in range(2):
        values = jnp.concatenate(
            [f_ref[:, member, 0, c].reshape(NY, NZ) for c in range(2)], axis=1
        )
        real, imag = long_transform(y_ref[...], values, -1)
        field = dot(three_terms(jnp.concatenate([real, imag], axis=1), 1), z_ref[...])
        real, imag = field[:, :NZ], field[:, NZ:]
        u_ref[member, 0, 0] = real
        u_ref[member, 1, 0] = imag
        source_re, source_im = w_ref[member, 0, 0], w_ref[member, 1, 0]
        term_re = real * source_re + imag * source_im
        term_im = real * source_im - imag * source_re
        term = real * real + imag * imag
        total_re = term_re if total_re is None else total_re + term_re
        total_im = term_im if total_im is None else total_im + term_im
        weight = term if weight is None else weight + term
    for kind, total in enumerate((total_re, total_im, weight)):
        total = total.reshape(ZH, YY, SHARE, NZ)
        for y in range(YY):
            sum_ref[lax.rem(y + YY - here, YY), :, kind, 0] = total[:, y]


def inverse(fields, sources, inside, start, count, z_dft, y_dft):
    return pl.pallas_call(
        inverse_kernel,
        grid=(count,),
        in_specs=[
            pl.BlockSpec((PARTS, 2, 1, 2, KY, NZ), lambda i: (0, 0, inside + i, 0, 0, 0)),
            pl.BlockSpec((2, 2, 1, NY, NZ), lambda i: (0, 0, start + i, 0, 0)),
            *[table_spec(t) for t in (z_dft, y_dft)],
        ],
        out_specs=[
            pl.BlockSpec((2, 2, 1, NY, NZ), lambda i: (0, 0, i, 0, 0)),
            pl.BlockSpec((YY, ZH, 3, 1, SHARE, NZ), lambda i: (0, 0, 0, i, 0, 0)),
        ],
        out_shape=[
            jax.ShapeDtypeStruct((2, 2, count, NY, NZ), jnp.float32),
            jax.ShapeDtypeStruct((YY, ZH, 3, count, SHARE, NZ), jnp.float32),
        ],
        compiler_params=pltpu.CompilerParams(vmem_limit_bytes=VMEM_LIMIT),
        cost_estimate=pl.CostEstimate(
            flops=600 * 10**6 * count, bytes_accessed=1900 * 1024 * count, transcendentals=0
        ),
        name="inverse_yz",
    )(fields, sources, z_dft, y_dft)


def update_kernel(*refs):
    parts, u_ref, w_ref, out_ref = refs[:YY], refs[YY], refs[YY + 1], refs[-1]
    here = lax.axis_index("y")
    for shift, part_ref in enumerate(parts):
        y = lax.rem(here + YY - shift, YY)
        for h in range(ZH):
            rows = pl.ds(pl.multiple_of((h * YY + y) * SHARE, SHARE), SHARE)
            real, imag = part_ref[h, 0, 0], part_ref[h, 1, 0]
            for member in range(2):
                field_re, field_im = u_ref[member, 0, 0, rows], u_ref[member, 1, 0, rows]
                scatter_re = real * field_re - imag * field_im
                scatter_im = real * field_im + imag * field_re
                out_ref[member, 0, 0, rows] = 0.5 * (w_ref[member, 0, 0, rows] + scatter_re)
                out_ref[member, 1, 0, rows] = 0.5 * (w_ref[member, 1, 0, rows] + scatter_im)


def update(parts, fields, sources, start, count, earlier):
    block = (2, 2, 1, NY, NZ)
    more = () if earlier is None else (earlier,)
    part_spec = pl.BlockSpec((ZH, 2, 1, SHARE, NZ), lambda i: (0, 0, i, 0, 0))
    return pl.pallas_call(
        update_kernel,
        grid=(count,),
        in_specs=[
            *[part_spec] * YY,
            pl.BlockSpec(block, lambda i: (0, 0, i, 0, 0)),
            pl.BlockSpec(block, lambda i: (0, 0, start + i, 0, 0)),
            *[pl.BlockSpec(memory_space=pl.ANY) for _ in more],
        ],
        out_specs=pl.BlockSpec(block, lambda i: (0, 0, start + i, 0, 0)),
        out_shape=jax.ShapeDtypeStruct(sources.shape, jnp.float32),
        input_output_aliases={YY + 2: 0} if more else {},
        compiler_params=pltpu.CompilerParams(vmem_limit_bytes=VMEM_LIMIT),
        cost_estimate=pl.CostEstimate(
            flops=10**6 * count, bytes_accessed=1800 * 1024 * count, transcendentals=0
        ),
        name="update",
    )(*parts, fields, sources, *more)


def exchange(values):
    return lax.all_to_all(values, PENCIL, split_axis=0, concat_axis=0, tiled=True)


def along_y(values, shift):
    return lax.ppermute(values, "y", [(i, (i + shift) % YY) for i in range(YY)])


def reduce_shots(sums):
    arrived = [along_y(sums[shift], shift) for shift in range(1, YY)]
    mine = sums[0] + arrived[0] + arrived[1] + arrived[2]
    both = mine + lax.ppermute(mine, "zh", [(0, 1), (1, 0)])
    return both[:, :2] / (1.0 + both[:, 2:])


def share_contrast(contrast):
    return [contrast, *[along_y(contrast, shift) for shift in range(1, YY)]]


CHUNKS = (4, 4)
PIECES = ((4,), (2, 2))


def shards(contrast_source, green_spectrum, source_cells):
    order = np.arange(NX).reshape(PARTS, PLANES).T.reshape(-1)
    y_dft = jnp.asarray(long_table())
    back_dft = jnp.asarray(long_table(order))
    z_forward = jnp.asarray(z_table(1))
    z_back = jnp.asarray(z_table(-1))

    images = []
    for member in range(2):
        spectra = exchange(forward(contrast_source, member, source_cells, z_forward, y_dft))
        images = spectral(spectra, green_spectrum, member, CHUNKS, y_dft, back_dft, images)
    updated = None
    shares = []
    start = 0
    parts = ()
    updates = []
    for image, pieces in zip(images, PIECES):
        fields, parts = lax.optimization_barrier((exchange(image), parts))
        inside = 0
        for count in pieces:
            field, sums = inverse(fields, contrast_source, inside, start, count, z_back, y_dft)
            contrast = reduce_shots(sums)
            shares.append(lax.dynamic_index_in_dim(contrast, lax.axis_index("zh"), 0, keepdims=False))
            parts = share_contrast(contrast)
            updates.append((parts, field, start, count))
            start += count
            inside += count
    for parts, field, start, count in updates:
        updated = update(parts, field, contrast_source, start, count, updated)
    return updated, jnp.concatenate(shares, axis=1)


def solution(mesh):
    fine = Mesh(mesh.devices.reshape(ZH, YY, 4, 4, 2), (*SHOT, *PENCIL))
    return jax.shard_map(
        shards,
        mesh=fine,
        in_specs=(
            P(SHOT, None, PENCIL, None, None),
            P(None, None, PENCIL, None),
            P(SHOT, None),
        ),
        out_specs=(P(SHOT, None, PENCIL, None, None), P(None, PENCIL, SHOT, None)),
        check_vma=False,
    )
```

```python
import functools
import math

import jax
import jax.numpy as jnp
import ml_dtypes
import numpy as np
from jax import lax
from jax.experimental import pallas as pl
from jax.experimental.pallas import tpu as pltpu
from jax.sharding import Mesh, PartitionSpec as P

SHOT = ("zh", "y")
PENCIL = ("zl", "x", "core")
ZH, YY = 2, 4
ZL, QUADS = 4, 8
PARTS = ZL * QUADS
NX, NY, NZ = 256, 256, 128
PLANES = NX // PARTS
KY = NY // PARTS
SHARE = NY // (ZH * YY)
GROUP = 4
FLOPS = 10**6
PARTNERS, WHOLE = -1, -2
VMEM_LIMIT = 60 * 1024 * 1024


def split_table(table):
    high = table.astype(ml_dtypes.bfloat16)
    return high, (table - high.astype(np.float64)).astype(ml_dtypes.bfloat16)


def cos_sin(length):
    index = np.arange(length)
    angle = 2.0 * np.pi * (index[:, None] * index[None, :] % length) / length
    return np.cos(angle) / math.sqrt(length), np.sin(angle) / math.sqrt(length)


def long_table(order=None):
    cosine, sine = cos_sin(NY)
    if order is not None:
        cosine, sine = cosine[order], sine[order]
    high, low = split_table(np.concatenate([cosine, sine], axis=0))
    return np.concatenate([high, high, low], axis=1)


def z_table(sign):
    cosine, sine = cos_sin(NZ)
    high, low = split_table(np.block([[cosine, -sign * sine], [sign * sine, cosine]]))
    return np.concatenate([high, high, low], axis=0)


def three_terms(values, axis):
    high = values.astype(jnp.bfloat16)
    low = (values - high.astype(jnp.float32)).astype(jnp.bfloat16)
    return jnp.concatenate([high, low, high], axis=axis)


def dot(left, right):
    return lax.dot_general(left, right, (((1,), (0,)), ((), ())), preferred_element_type=jnp.float32)


def long_transform(table, values, sign):
    both = dot(table, three_terms(values, 0))
    count, lanes = both.shape[0] // 2, both.shape[1] // 2
    cos_re, cos_im = both[:count, :lanes], both[:count, lanes:]
    sin_re, sin_im = both[count:, :lanes], both[count:, lanes:]
    if sign > 0:
        return cos_re + sin_im, cos_im - sin_re
    return cos_re - sin_im, cos_im + sin_re


ANY = pl.BlockSpec(memory_space=pl.ANY)


def quad_of(j):
    return lax.axis_index(("x", "core")) ^ j


def kernel_call(body, name, operands, out_shapes, scratch, flops, nbytes, aliases=None, smem=0):
    return pl.pallas_call(
        body,
        in_specs=[
            *[pl.BlockSpec(memory_space=pltpu.SMEM)] * smem,
            *[ANY] * (len(operands) - smem),
        ],
        out_specs=[ANY] * len(out_shapes),
        out_shape=[jax.ShapeDtypeStruct(shape, jnp.float32) for shape in out_shapes],
        scratch_shapes=scratch,
        input_output_aliases=aliases or {},
        compiler_params=pltpu.CompilerParams(vmem_limit_bytes=VMEM_LIMIT),
        cost_estimate=pl.CostEstimate(flops=flops, bytes_accessed=nbytes, transcendentals=0),
        name=name,
    )(*operands)


def table_scratch(*tables):
    return [pltpu.VMEM(t.shape, t.dtype) for t in tables]


def start_all(pairs, semaphores):
    copies = [
        pltpu.make_async_copy(source, target, semaphores.at[i])
        for i, (source, target) in enumerate(pairs)
    ]
    for copy in copies:
        copy.start()
    return copies


def wait_all(copies):
    for copy in copies:
        copy.wait()


def forward_kernel(member, staged, cell_ref, w_hbm, z_hbm, y_hbm, *refs):
    count = QUADS if staged else 1
    out_hbm = refs[:count]
    w_ref, z_ref, y_ref, out_ref, sem, out_sem = refs[count:]
    pairs = [(w_hbm.at[member, :, plane], w_ref.at[plane]) for plane in range(PLANES)]
    copies = start_all([*pairs, (z_hbm, z_ref), (y_hbm, y_ref)], sem)
    first_plane = lax.axis_index(PENCIL) * PLANES
    row = lax.broadcasted_iota(jnp.int32, (NY, NZ), 0)
    column = lax.broadcasted_iota(jnp.int32, (NY, NZ), 1)
    here = (row == cell_ref[member, 1]) & (column == cell_ref[member, 2])
    impulse = jnp.where(here, math.sqrt(NX * NY * NZ), 0.0)
    outs = []
    for group in range(PLANES // GROUP):
        planes = range(group * GROUP, (group + 1) * GROUP)
        wait_all([copies[plane] for plane in planes])
        if group == 0:
            wait_all(copies[PLANES:])
        for plane in planes:
            hit = (first_plane + plane == cell_ref[member, 0]).astype(jnp.float32)
            values = jnp.concatenate([w_ref[plane, 0] + hit * impulse, w_ref[plane, 1]], axis=1)
            values = dot(three_terms(values, 1), z_ref[...])
            real, imag = long_transform(y_ref[...], values, 1)
            out_ref[:, :, plane, 0] = real.reshape(ZL, QUADS, KY, NZ)
            out_ref[:, :, plane, 1] = imag.reshape(ZL, QUADS, KY, NZ)
        part = pl.ds(group * GROUP, GROUP)
        if staged:
            pairs = [
                (out_ref.at[:, quad_of(j), part], out.at[:, part]) for j, out in enumerate(out_hbm)
            ]
        else:
            pairs = [(out_ref.at[:, :, part], out_hbm[0].at[:, :, part])]
        outs += start_all(pairs, out_sem.at[pl.ds(group * count, count)])
    wait_all(outs)


def forward(source, member, staged, cells, z_dft, y_dft):
    shape = (ZL, QUADS, PLANES, 2, KY, NZ)
    return kernel_call(
        functools.partial(forward_kernel, member, staged),
        "forward_zy",
        (cells, source, z_dft, y_dft),
        [shape[:1] + shape[2:]] * QUADS if staged else [shape],
        [
            pltpu.VMEM((PLANES, 2, NY, NZ), jnp.float32),
            *table_scratch(z_dft, y_dft),
            pltpu.VMEM(shape, jnp.float32),
            pltpu.SemaphoreType.DMA((PLANES + 2,)),
            pltpu.SemaphoreType.DMA((PLANES // GROUP * (QUADS if staged else 1),)),
        ],
        FLOPS,
        5 * 2**20,
        smem=1,
    )


def spectral_kernel(chunks, forms, n_in, n_all, *refs):
    in_hbm, (green_hbm, x_hbm, back_hbm) = refs[:n_in], refs[n_in : n_in + 3]
    refs = refs[n_all:]
    n_out = sum(QUADS if form == PARTNERS else 1 for form in forms)
    out_hbm, refs = refs[:n_out], refs[n_out:]
    in_ref, green_ref, x_ref, back_ref, *out_refs, sem, out_sem = refs
    others = start_all([(x_hbm, x_ref), (green_hbm, green_ref), (back_hbm, back_ref)], sem)
    rows = PARTS * PLANES * 2 * KY // n_in
    inputs = start_all(
        [(hbm, in_ref.at[pl.ds(i * rows, rows)]) for i, hbm in enumerate(in_hbm)],
        sem.at[pl.ds(3, n_in)],
    )
    flat = [ref.reshape(PARTS * chunk * 2 * KY, NZ) for ref, chunk in zip(out_refs, chunks)]
    here = lax.axis_index(PENCIL)
    wait_all([others[0], *inputs])

    def take(c, ky):
        if n_in == 1:
            return in_ref[pl.ds(c * KY + ky, NX, stride=2 * KY), :]
        slots = [(here ^ part) * (PLANES * 2 * KY) for part in range(PARTS)]
        return jnp.concatenate(
            [in_ref[pl.ds(slot + c * KY + ky, PLANES, stride=2 * KY), :] for slot in slots], axis=0
        )

    for ky in range(KY):
        values = jnp.concatenate([take(c, ky) for c in range(2)], axis=1)
        real, imag = long_transform(x_ref[...], values, 1)
        if ky == 0:
            wait_all(others[1:])
        green_re = green_ref[pl.ds(ky, NX, stride=KY), :]
        green_im = green_ref[pl.ds(NX * KY + ky, NX, stride=KY), :]
        values = jnp.concatenate(
            [green_re * real - green_im * imag, green_re * imag + green_im * real], axis=1
        )
        results = long_transform(back_ref[...], values, -1)
        at = 0
        for chunk, out_ref in zip(chunks, flat):
            for plane in range(chunk):
                for c in range(2):
                    first = (plane * 2 + c) * KY + ky
                    out_ref[pl.ds(first, PARTS, stride=chunk * 2 * KY), :] = results[c][at : at + PARTS]
                at += PARTS
    pairs, at = [], 0
    for form, ref in zip(forms, out_refs):
        if form == PARTNERS:
            pairs += [(ref.at[:, quad_of(j)], out_hbm[at + j]) for j in range(QUADS)]
            at += QUADS
        else:
            target = out_hbm[at]
            pairs.append((ref, target if form == WHOLE else target.at[:, :, form]))
            at += 1
    wait_all(start_all(pairs, out_sem))


def spectral(spectra, green, chunks, forms, x_dft, back_dft, earlier=()):
    rows = 2 * KY * PARTS * PLANES
    spectra = [values.reshape(rows // len(spectra), NZ) for values in spectra]
    operands = (*spectra, green.reshape(2 * NX * KY, NZ), x_dft, back_dft, *earlier)
    shapes, aliases = [], {}
    for form, chunk in zip(forms, chunks):
        tail = (chunk, 2, KY, NZ)
        if form == PARTNERS:
            shapes += [(ZL, *tail)] * QUADS
        elif form == WHOLE:
            shapes.append((ZL, QUADS, *tail))
        else:
            if earlier:
                aliases[len(operands) - 1] = len(shapes)
            shapes.append((ZL, QUADS, 2, *tail))
    return kernel_call(
        functools.partial(spectral_kernel, chunks, forms, len(spectra), len(operands)),
        "spectral",
        operands,
        shapes,
        [
            pltpu.VMEM((rows, NZ), jnp.float32),
            pltpu.VMEM((2 * NX * KY, NZ), jnp.float32),
            *table_scratch(x_dft, back_dft),
            *[pltpu.VMEM((ZL, QUADS, chunk, 2, KY, NZ), jnp.float32) for chunk in chunks],
            pltpu.SemaphoreType.DMA((3 + len(spectra),)),
            pltpu.SemaphoreType.DMA((len(shapes),)),
        ],
        FLOPS,
        8 * 2**20,
        aliases=aliases,
    )


def pack_kernel(*refs):
    arrived, packed = refs[:QUADS], refs[QUADS : QUADS + ZL]
    held, sem, out_sem = refs[QUADS + ZL :]
    here = lax.axis_index("zl")
    wait_all(start_all([(ref, held.at[j]) for j, ref in enumerate(arrived)], sem))
    wait_all(start_all([(held.at[:, here ^ a], out) for a, out in enumerate(packed)], out_sem))


def over_quads(values):
    arrived = [
        values[0],
        *[
            lax.ppermute(values[j], ("x", "core"), [(i, i ^ j) for i in range(QUADS)])
            for j in range(1, QUADS)
        ],
    ]
    return kernel_call(
        pack_kernel,
        "pack",
        tuple(arrived),
        [(QUADS, *values[0].shape[1:])] * ZL,
        [
            pltpu.VMEM((QUADS, *values[0].shape), jnp.float32),
            pltpu.SemaphoreType.DMA((QUADS,)),
            pltpu.SemaphoreType.DMA((ZL,)),
        ],
        0,
        4 * 2**20,
    )


def over_z(values):
    return [
        values[0],
        *[
            lax.ppermute(values[a], "zl", [(i, i ^ a) for i in range(ZL)])
            for a in range(1, ZL)
        ],
    ]


def inverse_kernel(inside, start, count, n_in, *refs):
    f_hbm, refs = refs[:n_in], refs[n_in:]
    w_hbm, z_hbm, y_hbm, u_hbm, *refs = refs
    sum_hbm = refs[:YY]
    f_ref, w_ref, z_ref, y_ref, u_ref, sum_ref, sem, out_sem = refs[YY:]
    here = lax.axis_index("y")
    slots = [lax.axis_index(PENCIL) ^ part for part in range(PARTS)]
    tables = start_all([(y_hbm, y_ref), (z_hbm, z_ref)], sem)
    part = pl.ds(inside, count)
    if n_in == 1:
        pairs = [(f_hbm[0].at[:, member, part], f_ref.at[member]) for member in range(2)]
    else:
        pairs = [
            (f_hbm[a].at[:, part], f_ref.at[0, pl.ds(a * QUADS, QUADS)]) for a in range(ZL)
        ]
        pairs.append((f_hbm[ZL].at[:, part], f_ref.at[1]))
    inputs = start_all(pairs, sem.at[pl.ds(2, len(pairs))])
    sources = start_all(
        [(w_hbm.at[:, :, start + plane], w_ref.at[plane]) for plane in range(count)],
        sem.at[pl.ds(3 + ZL, count)],
    )
    wait_all([*tables, *inputs])
    for plane in range(count):
        for member in range(2):
            values = jnp.concatenate(
                [
                    f_ref[member, :, plane, c].reshape(NY, NZ)
                    if member == 1 or n_in == 1
                    else jnp.concatenate([f_ref[0, slot, plane, c] for slot in slots], axis=0)
                    for c in range(2)
                ],
                axis=1,
            )
            real, imag = long_transform(y_ref[...], values, -1)
            field = dot(three_terms(jnp.concatenate([real, imag], axis=1), 1), z_ref[...])
            u_ref[plane, member, 0] = field[:, :NZ]
            u_ref[plane, member, 1] = field[:, NZ:]
    wait_all(sources)
    for plane in range(count):
        for h in range(ZH):
            for y in range(YY):
                rows = pl.ds((h * YY + y) * SHARE, SHARE)
                totals = None
                for member in range(2):
                    real, imag = u_ref[plane, member, 0, rows], u_ref[plane, member, 1, rows]
                    source_re, source_im = w_ref[plane, member, 0, rows], w_ref[plane, member, 1, rows]
                    terms = (
                        real * source_re + imag * source_im,
                        real * source_im - imag * source_re,
                        real * real + imag * imag,
                    )
                    totals = terms if totals is None else [a + b for a, b in zip(totals, terms)]
                for kind in range(3):
                    sum_ref[y, h, kind, plane] = totals[kind]
    outs = start_all(
        [(sum_ref.at[lax.rem(here + shift, YY)], sum_hbm[shift]) for shift in range(YY)], out_sem
    )
    outs += start_all([(u_ref, u_hbm)], out_sem.at[pl.ds(YY, 1)])
    wait_all(outs)


def inverse(fields, sources, inside, start, count, z_dft, y_dft):
    sum_shape = (ZH, 3, count, SHARE, NZ)
    u_shape = (count, 2, 2, NY, NZ)
    outs = kernel_call(
        functools.partial(inverse_kernel, inside, start, count, len(fields)),
        "inverse_yz",
        (*fields, sources, z_dft, y_dft),
        [u_shape, *[sum_shape] * YY],
        [
            pltpu.VMEM((2, PARTS, count, 2, KY, NZ), jnp.float32),
            pltpu.VMEM(u_shape, jnp.float32),
            *table_scratch(z_dft, y_dft),
            pltpu.VMEM(u_shape, jnp.float32),
            pltpu.VMEM((YY, *sum_shape), jnp.float32),
            pltpu.SemaphoreType.DMA((3 + ZL + count,)),
            pltpu.SemaphoreType.DMA((YY + 1,)),
        ],
        FLOPS,
        4 * 2**20 * count // 2,
    )
    return outs[0], outs[1:]


def update_kernel(*refs):
    parts, u_ref, w_ref, out_ref = refs[:YY], refs[YY], refs[YY + 1], refs[-1]
    here = lax.axis_index("y")
    for shift, part_ref in enumerate(parts):
        y = lax.rem(here + YY - shift, YY)
        for h in range(ZH):
            rows = pl.ds(pl.multiple_of((h * YY + y) * SHARE, SHARE), SHARE)
            real, imag = part_ref[h, 0, 0], part_ref[h, 1, 0]
            for member in range(2):
                field_re, field_im = u_ref[0, member, 0, rows], u_ref[0, member, 1, rows]
                scatter_re = real * field_re - imag * field_im
                scatter_im = real * field_im + imag * field_re
                out_ref[member, 0, 0, rows] = 0.5 * (w_ref[member, 0, 0, rows] + scatter_re)
                out_ref[member, 1, 0, rows] = 0.5 * (w_ref[member, 1, 0, rows] + scatter_im)


def update(parts, fields, sources, start, count, earlier):
    block = (2, 2, 1, NY, NZ)
    more = () if earlier is None else (earlier,)
    part_spec = pl.BlockSpec((ZH, 2, 1, SHARE, NZ), lambda i: (0, 0, i, 0, 0))
    return pl.pallas_call(
        update_kernel,
        grid=(count,),
        in_specs=[
            *[part_spec] * YY,
            pl.BlockSpec((1, 2, 2, NY, NZ), lambda i: (i, 0, 0, 0, 0)),
            pl.BlockSpec(block, lambda i: (0, 0, start + i, 0, 0)),
            *[pl.BlockSpec(memory_space=pl.ANY) for _ in more],
        ],
        out_specs=pl.BlockSpec(block, lambda i: (0, 0, start + i, 0, 0)),
        out_shape=jax.ShapeDtypeStruct(sources.shape, jnp.float32),
        input_output_aliases={YY + 2: 0} if more else {},
        compiler_params=pltpu.CompilerParams(vmem_limit_bytes=VMEM_LIMIT),
        cost_estimate=pl.CostEstimate(
            flops=FLOPS, bytes_accessed=1800 * 1024 * count, transcendentals=0
        ),
        name="update",
    )(*parts, fields, sources, *more)


def exchange(values):
    return lax.all_to_all(values, PENCIL, split_axis=0, concat_axis=0, tiled=True)


def along_y(values, shift):
    return lax.ppermute(values, "y", [(i, (i + shift) % YY) for i in range(YY)])


def reduce_y(sums):
    arrived = [along_y(sums[shift], shift) for shift in range(1, YY)]
    return sums[0] + arrived[0] + arrived[1] + arrived[2]


def contrast_of(mine):
    both = mine + lax.ppermute(mine, "zh", [(0, 1), (1, 0)])
    return both[:, :2] / (1.0 + both[:, 2:])


def share_contrast(contrast):
    return [contrast, *[along_y(contrast, shift) for shift in range(1, YY)]]


CHUNKS = (4, 4)
PIECES = ((2, 2), (2, 2))


def shards(contrast_source, green_spectrum, source_cells):
    order = np.arange(NX).reshape(PARTS, PLANES).T.reshape(-1)
    y_dft = jnp.asarray(long_table())
    back_dft = jnp.asarray(long_table(order))
    z_forward = jnp.asarray(z_table(1))
    z_back = jnp.asarray(z_table(-1))

    spectra = []
    for member in range(2):
        (values,) = forward(contrast_source, member, False, source_cells, z_forward, y_dft)
        spectra.append([exchange(values.reshape(PARTS, PLANES, 2, KY, NZ))])
    *early, both = spectral(
        spectra[0], green_spectrum, CHUNKS, (PARTNERS, 0), y_dft, back_dft
    )
    early = over_quads(early)
    spectra[1], early = lax.optimization_barrier((spectra[1], early))
    early = over_z(early)
    single, both = spectral(
        spectra[1], green_spectrum, CHUNKS, (WHOLE, 1), y_dft, back_dft, (both,)
    )
    early, single = lax.optimization_barrier((early, single))
    single = exchange(single.reshape(PARTS, CHUNKS[0], 2, KY, NZ))
    both = exchange(both.reshape(PARTS, 2, CHUNKS[1], 2, KY, NZ))

    shares, updates, earlier = [], [], []
    start = 0
    for fields, pieces in zip(((*early, single), (both,)), PIECES):
        fields, earlier = lax.optimization_barrier((fields, earlier))
        inside = 0
        for count in pieces:
            field, sums = inverse(
                fields, contrast_source, inside, start, count, z_back, y_dft
            )
            mine = reduce_y(sums)
            if earlier and inside + count == sum(pieces):
                mine, earlier = lax.optimization_barrier((mine, earlier))
                updates[: len(earlier)] = [
                    (part, *update[1:]) for part, update in zip(earlier, updates)
                ]
                earlier = []
            contrast = contrast_of(mine)
            shares.append(lax.dynamic_index_in_dim(contrast, lax.axis_index("zh"), 0, keepdims=False))
            updates.append((share_contrast(contrast), field, start, count))
            start += count
            inside += count
        earlier = [update[0] for update in updates]
    updated = None
    for parts, field, start, count in updates:
        updated = update(parts, field, contrast_source, start, count, updated)
    return updated, jnp.concatenate(shares, axis=1)


def solution(mesh):
    fine = Mesh(mesh.devices.reshape(ZH, YY, 4, 4, 2), (*SHOT, *PENCIL))
    return jax.shard_map(
        shards,
        mesh=fine,
        in_specs=(
            P(SHOT, None, PENCIL, None, None),
            P(None, None, PENCIL, None),
            P(SHOT, None),
        ),
        out_specs=(P(SHOT, None, PENCIL, None, None), P(None, PENCIL, SHOT, None)),
        check_vma=False,
    )
```

```python
import functools
import math

import jax
import jax.numpy as jnp
import ml_dtypes
import numpy as np
from jax import lax
from jax.experimental import pallas as pl
from jax.experimental.pallas import tpu as pltpu
from jax.sharding import Mesh, PartitionSpec as P

SHOT = ("zh", "y")
PENCIL = ("zl", "x", "core")
ZH, YY = 2, 4
ZL, QUADS = 4, 8
PARTS = ZL * QUADS
NX, NY, NZ = 256, 256, 128
PLANES = NX // PARTS
KY = NY // PARTS
SHARE = NY // (ZH * YY)
GROUP = 4
FLOPS = 10**6
PARTNERS, WHOLE = -1, -2
VMEM_LIMIT = 60 * 1024 * 1024


def split_table(table):
    high = table.astype(ml_dtypes.bfloat16)
    return high, (table - high.astype(np.float64)).astype(ml_dtypes.bfloat16)


def cos_sin(length):
    index = np.arange(length)
    angle = 2.0 * np.pi * (index[:, None] * index[None, :] % length) / length
    return np.cos(angle) / math.sqrt(length), np.sin(angle) / math.sqrt(length)


def long_table(order=None):
    cosine, sine = cos_sin(NY)
    if order is not None:
        cosine, sine = cosine[order], sine[order]
    high, low = split_table(np.concatenate([cosine, sine], axis=0))
    return np.concatenate([high, high, low], axis=1)


def z_table(sign):
    cosine, sine = cos_sin(NZ)
    high, low = split_table(np.block([[cosine, -sign * sine], [sign * sine, cosine]]))
    return np.concatenate([high, high, low], axis=0)


def three_terms(values, axis):
    high = values.astype(jnp.bfloat16)
    low = (values - high.astype(jnp.float32)).astype(jnp.bfloat16)
    return jnp.concatenate([high, low, high], axis=axis)


def dot(left, right):
    return lax.dot_general(left, right, (((1,), (0,)), ((), ())), preferred_element_type=jnp.float32)


def long_transform(table, values, sign):
    both = dot(table, three_terms(values, 0))
    count, lanes = both.shape[0] // 2, both.shape[1] // 2
    cos_re, cos_im = both[:count, :lanes], both[:count, lanes:]
    sin_re, sin_im = both[count:, :lanes], both[count:, lanes:]
    if sign > 0:
        return cos_re + sin_im, cos_im - sin_re
    return cos_re - sin_im, cos_im + sin_re


ANY = pl.BlockSpec(memory_space=pl.ANY)


def quad_of(j):
    return lax.axis_index(("x", "core")) ^ j


def kernel_call(body, name, operands, out_shapes, scratch, flops, nbytes, aliases=None, smem=0):
    return pl.pallas_call(
        body,
        in_specs=[
            *[pl.BlockSpec(memory_space=pltpu.SMEM)] * smem,
            *[ANY] * (len(operands) - smem),
        ],
        out_specs=[ANY] * len(out_shapes),
        out_shape=[jax.ShapeDtypeStruct(shape, jnp.float32) for shape in out_shapes],
        scratch_shapes=scratch,
        input_output_aliases=aliases or {},
        compiler_params=pltpu.CompilerParams(vmem_limit_bytes=VMEM_LIMIT),
        cost_estimate=pl.CostEstimate(flops=flops, bytes_accessed=nbytes, transcendentals=0),
        name=name,
    )(*operands)


def table_scratch(*tables):
    return [pltpu.VMEM(t.shape, t.dtype) for t in tables]


def start_all(pairs, semaphores):
    copies = [
        pltpu.make_async_copy(source, target, semaphores.at[i])
        for i, (source, target) in enumerate(pairs)
    ]
    for copy in copies:
        copy.start()
    return copies


def wait_all(copies):
    for copy in copies:
        copy.wait()


def forward_kernel(member, early, cell_ref, w_hbm, z_hbm, y_hbm, *refs):
    n_out = (QUADS if early else 0) + 1
    *early_hbm, whole_hbm = refs[:n_out]
    w_ref, z_ref, y_ref, out_ref, sem, out_sem = refs[n_out:]
    pairs = [(w_hbm.at[member, :, plane], w_ref.at[plane]) for plane in range(PLANES)]
    copies = start_all([*pairs, (z_hbm, z_ref), (y_hbm, y_ref)], sem)
    first_plane = lax.axis_index(PENCIL) * PLANES
    row = lax.broadcasted_iota(jnp.int32, (NY, NZ), 0)
    column = lax.broadcasted_iota(jnp.int32, (NY, NZ), 1)
    here = (row == cell_ref[member, 1]) & (column == cell_ref[member, 2])
    impulse = jnp.where(here, math.sqrt(NX * NY * NZ), 0.0)
    outs = []
    for group in range(PLANES // GROUP):
        planes = range(group * GROUP, (group + 1) * GROUP)
        wait_all([copies[plane] for plane in planes])
        if group == 0:
            wait_all(copies[PLANES:])
        for plane in planes:
            hit = (first_plane + plane == cell_ref[member, 0]).astype(jnp.float32)
            values = jnp.concatenate([w_ref[plane, 0] + hit * impulse, w_ref[plane, 1]], axis=1)
            values = dot(three_terms(values, 1), z_ref[...])
            real, imag = long_transform(y_ref[...], values, 1)
            out_ref[:, :, plane, 0] = real.reshape(ZL, QUADS, KY, NZ)
            out_ref[:, :, plane, 1] = imag.reshape(ZL, QUADS, KY, NZ)
        first = group * GROUP
        pairs = []
        if group == 0:
            pairs = [
                (out_ref.at[:, quad_of(j), pl.ds(0, early)], out) for j, out in enumerate(early_hbm)
            ]
            first = early
        count = (group + 1) * GROUP - first
        pairs.append(
            (out_ref.at[:, :, pl.ds(first, count)], whole_hbm.at[:, :, pl.ds(first - early, count)])
        )
        outs += start_all(pairs, out_sem.at[pl.ds(0 if group == 0 else n_out + group - 1, len(pairs))])
    wait_all(outs)


def forward(source, member, early, cells, z_dft, y_dft):
    shapes = [(ZL, early, 2, KY, NZ)] * QUADS if early else []
    return kernel_call(
        functools.partial(forward_kernel, member, early),
        "forward_zy",
        (cells, source, z_dft, y_dft),
        [*shapes, (ZL, QUADS, PLANES - early, 2, KY, NZ)],
        [
            pltpu.VMEM((PLANES, 2, NY, NZ), jnp.float32),
            *table_scratch(z_dft, y_dft),
            pltpu.VMEM((ZL, QUADS, PLANES, 2, KY, NZ), jnp.float32),
            pltpu.SemaphoreType.DMA((PLANES + 2,)),
            pltpu.SemaphoreType.DMA((len(shapes) + PLANES // GROUP,)),
        ],
        FLOPS,
        5 * 2**20,
        smem=1,
    )


def spectral_kernel(chunks, forms, n_in, n_all, *refs):
    in_hbm, (green_hbm, x_hbm, back_hbm) = refs[:n_in], refs[n_in : n_in + 3]
    refs = refs[n_all:]
    n_out = sum(QUADS if form == PARTNERS else 1 for form in forms)
    out_hbm, refs = refs[:n_out], refs[n_out:]
    in_ref, green_ref, x_ref, back_ref, *out_refs, sem, out_sem = refs
    others = start_all([(x_hbm, x_ref), (green_hbm, green_ref), (back_hbm, back_ref)], sem)
    here = lax.axis_index(PENCIL)
    *slots, whole = in_hbm
    early = slots[0].shape[1] if slots else 0
    pairs = [(whole, in_ref.at[:, pl.ds(early, PLANES - early)])]
    for a, slot in enumerate(slots):
        for j in range(QUADS):
            pairs.append((slot.at[j], in_ref.at[here ^ (a * QUADS + j), pl.ds(0, early)]))
    inputs = start_all(pairs, sem.at[pl.ds(3, len(pairs))])
    flat = [ref.reshape(PARTS * chunk * 2 * KY, NZ) for ref, chunk in zip(out_refs, chunks)]
    flat_in = in_ref.reshape(PARTS * PLANES * 2 * KY, NZ)
    wait_all([others[0], *inputs])

    def take(c, ky):
        return flat_in[pl.ds(c * KY + ky, NX, stride=2 * KY), :]

    for ky in range(KY):
        values = jnp.concatenate([take(c, ky) for c in range(2)], axis=1)
        real, imag = long_transform(x_ref[...], values, 1)
        if ky == 0:
            wait_all(others[1:])
        green_re = green_ref[pl.ds(ky, NX, stride=KY), :]
        green_im = green_ref[pl.ds(NX * KY + ky, NX, stride=KY), :]
        values = jnp.concatenate(
            [green_re * real - green_im * imag, green_re * imag + green_im * real], axis=1
        )
        results = long_transform(back_ref[...], values, -1)
        at = 0
        for chunk, out_ref in zip(chunks, flat):
            for plane in range(chunk):
                for c in range(2):
                    first = (plane * 2 + c) * KY + ky
                    out_ref[pl.ds(first, PARTS, stride=chunk * 2 * KY), :] = results[c][at : at + PARTS]
                at += PARTS
    pairs, at = [], 0
    for form, ref in zip(forms, out_refs):
        if form == PARTNERS:
            pairs += [(ref.at[:, quad_of(j)], out_hbm[at + j]) for j in range(QUADS)]
            at += QUADS
        else:
            target = out_hbm[at]
            pairs.append((ref, target if form == WHOLE else target.at[:, :, form]))
            at += 1
    wait_all(start_all(pairs, out_sem))


def spectral(spectra, green, chunks, forms, x_dft, back_dft, earlier=()):
    operands = (*spectra, green.reshape(2 * NX * KY, NZ), x_dft, back_dft, *earlier)
    shapes, aliases = [], {}
    for form, chunk in zip(forms, chunks):
        tail = (chunk, 2, KY, NZ)
        if form == PARTNERS:
            shapes += [(ZL, *tail)] * QUADS
        elif form == WHOLE:
            shapes.append((ZL, QUADS, *tail))
        else:
            if earlier:
                aliases[len(operands) - 1] = len(shapes)
            shapes.append((ZL, QUADS, 2, *tail))
    return kernel_call(
        functools.partial(spectral_kernel, chunks, forms, len(spectra), len(operands)),
        "spectral",
        operands,
        shapes,
        [
            pltpu.VMEM((PARTS, PLANES, 2, KY, NZ), jnp.float32),
            pltpu.VMEM((2 * NX * KY, NZ), jnp.float32),
            *table_scratch(x_dft, back_dft),
            *[pltpu.VMEM((ZL, QUADS, chunk, 2, KY, NZ), jnp.float32) for chunk in chunks],
            pltpu.SemaphoreType.DMA((4 + (PARTS if len(spectra) > 1 else 0),)),
            pltpu.SemaphoreType.DMA((len(shapes),)),
        ],
        FLOPS,
        8 * 2**20,
        aliases=aliases,
    )


def pack_kernel(*refs):
    arrived, packed = refs[:QUADS], refs[QUADS : QUADS + ZL]
    held, sem, out_sem = refs[QUADS + ZL :]
    here = lax.axis_index("zl")
    wait_all(start_all([(ref, held.at[j]) for j, ref in enumerate(arrived)], sem))
    wait_all(start_all([(held.at[:, here ^ a], out) for a, out in enumerate(packed)], out_sem))


def over_quads(values):
    arrived = [
        values[0],
        *[
            lax.ppermute(values[j], ("x", "core"), [(i, i ^ j) for i in range(QUADS)])
            for j in range(1, QUADS)
        ],
    ]
    return kernel_call(
        pack_kernel,
        "pack",
        tuple(arrived),
        [(QUADS, *values[0].shape[1:])] * ZL,
        [
            pltpu.VMEM((QUADS, *values[0].shape), jnp.float32),
            pltpu.SemaphoreType.DMA((QUADS,)),
            pltpu.SemaphoreType.DMA((ZL,)),
        ],
        0,
        4 * 2**20,
    )


def over_z(values):
    return [
        values[0],
        *[
            lax.ppermute(values[a], "zl", [(i, i ^ a) for i in range(ZL)])
            for a in range(1, ZL)
        ],
    ]


def inverse_kernel(inside, start, count, n_in, *refs):
    f_hbm, refs = refs[:n_in], refs[n_in:]
    w_hbm, z_hbm, y_hbm, u_hbm, *refs = refs
    sum_hbm = refs[:YY]
    f_ref, w_ref, z_ref, y_ref, u_ref, sum_ref, sem, out_sem = refs[YY:]
    here = lax.axis_index("y")
    slots = [lax.axis_index(PENCIL) ^ part for part in range(PARTS)]
    tables = start_all([(y_hbm, y_ref), (z_hbm, z_ref)], sem)
    part = pl.ds(inside, count)
    if n_in == 1:
        pairs = [(f_hbm[0].at[:, member, part], f_ref.at[member]) for member in range(2)]
    else:
        pairs = [
            (f_hbm[a].at[:, part], f_ref.at[0, pl.ds(a * QUADS, QUADS)]) for a in range(ZL)
        ]
        pairs.append((f_hbm[ZL].at[:, part], f_ref.at[1]))
    inputs = start_all(pairs, sem.at[pl.ds(2, len(pairs))])
    sources = start_all(
        [(w_hbm.at[:, :, start + plane], w_ref.at[plane]) for plane in range(count)],
        sem.at[pl.ds(3 + ZL, count)],
    )
    wait_all([*tables, *inputs])
    for plane in range(count):
        for member in range(2):
            values = jnp.concatenate(
                [
                    f_ref[member, :, plane, c].reshape(NY, NZ)
                    if member == 1 or n_in == 1
                    else jnp.concatenate([f_ref[0, slot, plane, c] for slot in slots], axis=0)
                    for c in range(2)
                ],
                axis=1,
            )
            real, imag = long_transform(y_ref[...], values, -1)
            field = dot(three_terms(jnp.concatenate([real, imag], axis=1), 1), z_ref[...])
            u_ref[plane, member, 0] = field[:, :NZ]
            u_ref[plane, member, 1] = field[:, NZ:]
    wait_all(sources)
    for plane in range(count):
        for h in range(ZH):
            for y in range(YY):
                rows = pl.ds((h * YY + y) * SHARE, SHARE)
                totals = None
                for member in range(2):
                    real, imag = u_ref[plane, member, 0, rows], u_ref[plane, member, 1, rows]
                    source_re, source_im = w_ref[plane, member, 0, rows], w_ref[plane, member, 1, rows]
                    terms = (
                        real * source_re + imag * source_im,
                        real * source_im - imag * source_re,
                        real * real + imag * imag,
                    )
                    totals = terms if totals is None else [a + b for a, b in zip(totals, terms)]
                for kind in range(3):
                    sum_ref[y, h, kind, plane] = totals[kind]
    outs = start_all(
        [(sum_ref.at[lax.rem(here + shift, YY)], sum_hbm[shift]) for shift in range(YY)], out_sem
    )
    outs += start_all([(u_ref, u_hbm)], out_sem.at[pl.ds(YY, 1)])
    wait_all(outs)


def inverse(fields, sources, inside, start, count, z_dft, y_dft):
    sum_shape = (ZH, 3, count, SHARE, NZ)
    u_shape = (count, 2, 2, NY, NZ)
    outs = kernel_call(
        functools.partial(inverse_kernel, inside, start, count, len(fields)),
        "inverse_yz",
        (*fields, sources, z_dft, y_dft),
        [u_shape, *[sum_shape] * YY],
        [
            pltpu.VMEM((2, PARTS, count, 2, KY, NZ), jnp.float32),
            pltpu.VMEM(u_shape, jnp.float32),
            *table_scratch(z_dft, y_dft),
            pltpu.VMEM(u_shape, jnp.float32),
            pltpu.VMEM((YY, *sum_shape), jnp.float32),
            pltpu.SemaphoreType.DMA((3 + ZL + count,)),
            pltpu.SemaphoreType.DMA((YY + 1,)),
        ],
        FLOPS,
        4 * 2**20 * count // 2,
    )
    return outs[0], outs[1:]


def update_kernel(*refs):
    parts, u_ref, w_ref, out_ref = refs[:YY], refs[YY], refs[YY + 1], refs[-1]
    here = lax.axis_index("y")
    for shift, part_ref in enumerate(parts):
        y = lax.rem(here + YY - shift, YY)
        for h in range(ZH):
            rows = pl.ds(pl.multiple_of((h * YY + y) * SHARE, SHARE), SHARE)
            real, imag = part_ref[h, 0, 0], part_ref[h, 1, 0]
            for member in range(2):
                field_re, field_im = u_ref[0, member, 0, rows], u_ref[0, member, 1, rows]
                scatter_re = real * field_re - imag * field_im
                scatter_im = real * field_im + imag * field_re
                out_ref[member, 0, 0, rows] = 0.5 * (w_ref[member, 0, 0, rows] + scatter_re)
                out_ref[member, 1, 0, rows] = 0.5 * (w_ref[member, 1, 0, rows] + scatter_im)


def update(parts, fields, sources, start, count, earlier):
    block = (2, 2, 1, NY, NZ)
    more = () if earlier is None else (earlier,)
    part_spec = pl.BlockSpec((ZH, 2, 1, SHARE, NZ), lambda i: (0, 0, i, 0, 0))
    return pl.pallas_call(
        update_kernel,
        grid=(count,),
        in_specs=[
            *[part_spec] * YY,
            pl.BlockSpec((1, 2, 2, NY, NZ), lambda i: (i, 0, 0, 0, 0)),
            pl.BlockSpec(block, lambda i: (0, 0, start + i, 0, 0)),
            *[pl.BlockSpec(memory_space=pl.ANY) for _ in more],
        ],
        out_specs=pl.BlockSpec(block, lambda i: (0, 0, start + i, 0, 0)),
        out_shape=jax.ShapeDtypeStruct(sources.shape, jnp.float32),
        input_output_aliases={YY + 2: 0} if more else {},
        compiler_params=pltpu.CompilerParams(vmem_limit_bytes=VMEM_LIMIT),
        cost_estimate=pl.CostEstimate(
            flops=FLOPS, bytes_accessed=1800 * 1024 * count, transcendentals=0
        ),
        name="update",
    )(*parts, fields, sources, *more)


def exchange(values):
    return lax.all_to_all(values, PENCIL, split_axis=0, concat_axis=0, tiled=True)


def along_y(values, shift):
    return lax.ppermute(values, "y", [(i, (i + shift) % YY) for i in range(YY)])


def reduce_y(sums):
    arrived = [along_y(sums[shift], shift) for shift in range(1, YY)]
    return sums[0] + arrived[0] + arrived[1] + arrived[2]


def contrast_of(mine, earlier):
    other = lax.ppermute(mine, "zh", [(0, 1), (1, 0)])
    both = mine + (after(other, earlier) if earlier else other)
    return both[:, :2] / (1.0 + both[:, 2:])


def share_contrast(contrast):
    return [contrast, *[along_y(contrast, shift) for shift in range(1, YY)]]


CHUNKS = (4, 4)
PIECES = ((2, 2), (2, 2))


EARLY = (0, 0)


def after(values, others):
    return lax.optimization_barrier((values, others))[0]


def shards(contrast_source, green_spectrum, source_cells):
    order = np.arange(NX).reshape(PARTS, PLANES).T.reshape(-1)
    y_dft = jnp.asarray(long_table())
    back_dft = jnp.asarray(long_table(order))
    z_forward = jnp.asarray(z_table(1))
    z_back = jnp.asarray(z_table(-1))

    spectra, parted = [], []
    for member in range(2):
        *partners, whole = forward(
            contrast_source, member, EARLY[member], source_cells, z_forward, y_dft
        )
        if partners:
            partners = over_quads(partners)
            whole = after(whole, partners)
            parted = over_z(partners)
        whole = exchange(whole.reshape(PARTS, PLANES - EARLY[member], 2, KY, NZ))
        spectra.append(whole)
    *early, both = spectral(
        [after(spectra[0], parted) if parted else spectra[0]], green_spectrum, CHUNKS, (PARTNERS, 0), y_dft, back_dft
    )
    early = over_quads(early)
    whole = after(spectra[1], early)
    early = over_z(early)
    single, both = spectral(
        [*parted, whole], green_spectrum, CHUNKS, (WHOLE, 1), y_dft, back_dft, (both,)
    )
    single = exchange(after(single, early).reshape(PARTS, CHUNKS[0], 2, KY, NZ))
    both = exchange(both.reshape(PARTS, 2, CHUNKS[1], 2, KY, NZ))

    def part_of(fields, inside, start, count, before_sums, before_contrast):
        field, sums = inverse(fields, contrast_source, inside, start, count, z_back, y_dft)
        mine, before_sums = lax.optimization_barrier((reduce_y(sums), before_sums))
        contrast = contrast_of(mine, before_contrast)
        share = lax.dynamic_index_in_dim(contrast, lax.axis_index("zh"), 0, keepdims=False)
        return share, (share_contrast(contrast), field), before_sums

    def renew(pair, start, count, updated):
        return update(*pair, contrast_source, start, count, updated)

    (a1, a2), (b1, b2) = PIECES
    first, second = (*early, single), (both,)
    share_a1, pair_a1, _ = part_of(first, 0, 0, a1, (), None)
    share_a2, pair_a2, _ = part_of(first, a1, a1, a2, (), None)
    updated = renew(pair_a1, 0, a1, None)
    second, updated, pair_a2 = lax.optimization_barrier((second, updated, pair_a2))
    share_b1, pair_b1, _ = part_of(second, 0, a1 + a2, b1, (), None)
    share_b2, pair_b2, pair_a2 = part_of(second, b1, a1 + a2 + b1, b2, pair_a2, pair_b1[0])
    updated = renew(pair_a2, a1, a2, updated)
    updated = renew(pair_b1, a1 + a2, b1, updated)
    updated = renew(pair_b2, a1 + a2 + b1, b2, updated)
    return updated, jnp.concatenate([share_a1, share_a2, share_b1, share_b2], axis=1)


def solution(mesh):
    fine = Mesh(mesh.devices.reshape(ZH, YY, 4, 4, 2), (*SHOT, *PENCIL))
    return jax.shard_map(
        shards,
        mesh=fine,
        in_specs=(
            P(SHOT, None, PENCIL, None, None),
            P(None, None, PENCIL, None),
            P(SHOT, None),
        ),
        out_specs=(P(SHOT, None, PENCIL, None, None), P(None, PENCIL, SHOT, None)),
        check_vma=False,
    )
```

```python
import functools
import math

import jax
import jax.numpy as jnp
import ml_dtypes
import numpy as np
from jax import lax
from jax.experimental import pallas as pl
from jax.experimental.pallas import tpu as pltpu
from jax.sharding import Mesh, PartitionSpec as P

SHOT = ("zh", "y")
PENCIL = ("zl", "x", "core")
ZH, YY = 2, 4
ZL, QUADS = 4, 8
PARTS = ZL * QUADS
NX, NY, NZ = 256, 256, 128
PLANES = NX // PARTS
KY = NY // PARTS
SHARE = NY // (ZH * YY)
GROUPS = ((0, 2), (2, 4), (6, 2))
FLOPS = 10**6
PARTNERS, WHOLE = -1, -2
VMEM_LIMIT = 62 * 1024 * 1024


def split_table(table):
    high = table.astype(ml_dtypes.bfloat16)
    return high, (table - high.astype(np.float64)).astype(ml_dtypes.bfloat16)


def cos_sin(length):
    index = np.arange(length)
    angle = 2.0 * np.pi * (index[:, None] * index[None, :] % length) / length
    return np.cos(angle) / math.sqrt(length), np.sin(angle) / math.sqrt(length)


def long_table(order=None):
    cosine, sine = cos_sin(NY)
    if order is not None:
        cosine, sine = cosine[order], sine[order]
    high, low = split_table(np.concatenate([cosine, sine], axis=0))
    return np.concatenate([high, high, low], axis=1)


def z_table(sign):
    cosine, sine = cos_sin(NZ)
    high, low = split_table(np.block([[cosine, -sign * sine], [sign * sine, cosine]]))
    return np.concatenate([high, high, low], axis=0)


def three_terms(values, axis):
    high = values.astype(jnp.bfloat16)
    low = (values - high.astype(jnp.float32)).astype(jnp.bfloat16)
    return jnp.concatenate([high, low, high], axis=axis)


def dot(left, right):
    return lax.dot_general(left, right, (((1,), (0,)), ((), ())), preferred_element_type=jnp.float32)


def long_transform(table, values, sign):
    both = dot(table, three_terms(values, 0))
    count, lanes = both.shape[0] // 2, both.shape[1] // 2
    cos_re, cos_im = both[:count, :lanes], both[:count, lanes:]
    sin_re, sin_im = both[count:, :lanes], both[count:, lanes:]
    if sign > 0:
        return cos_re + sin_im, cos_im - sin_re
    return cos_re - sin_im, cos_im + sin_re


ANY = pl.BlockSpec(memory_space=pl.ANY)


def quad_of(j):
    return lax.axis_index(("x", "core")) ^ j


def kernel_call(body, name, operands, out_shapes, scratch, flops, nbytes, aliases=None, smem=0):
    return pl.pallas_call(
        body,
        in_specs=[
            *[pl.BlockSpec(memory_space=pltpu.SMEM)] * smem,
            *[ANY] * (len(operands) - smem),
        ],
        out_specs=[ANY] * len(out_shapes),
        out_shape=[jax.ShapeDtypeStruct(shape, jnp.float32) for shape in out_shapes],
        scratch_shapes=scratch,
        input_output_aliases=aliases or {},
        compiler_params=pltpu.CompilerParams(vmem_limit_bytes=VMEM_LIMIT),
        cost_estimate=pl.CostEstimate(flops=flops, bytes_accessed=nbytes, transcendentals=0),
        name=name,
    )(*operands)


def table_scratch(*tables):
    return [pltpu.VMEM(t.shape, t.dtype) for t in tables]


def start_all(pairs, semaphores):
    copies = [
        pltpu.make_async_copy(source, target, semaphores.at[i])
        for i, (source, target) in enumerate(pairs)
    ]
    for copy in copies:
        copy.start()
    return copies


def wait_all(copies):
    for copy in copies:
        copy.wait()


def forward_kernel(
    member, cell_ref, w_hbm, z_hbm, y_hbm, out_hbm, w_ref, z_ref, y_ref, out_ref, sem, out_sem
):
    pairs = [(w_hbm.at[member, :, plane], w_ref.at[plane]) for plane in range(PLANES)]
    tables = start_all([(z_hbm, z_ref), (y_hbm, y_ref)], sem.at[pl.ds(PLANES, 2)])
    copies = [*start_all(pairs, sem.at[pl.ds(0, PLANES)]), *tables]
    first_plane = lax.axis_index(PENCIL) * PLANES
    row = lax.broadcasted_iota(jnp.int32, (NY, NZ), 0)
    column = lax.broadcasted_iota(jnp.int32, (NY, NZ), 1)
    here = (row == cell_ref[member, 1]) & (column == cell_ref[member, 2])
    impulse = jnp.where(here, math.sqrt(NX * NY * NZ), 0.0)
    outs = []
    for group, (first, count) in enumerate(GROUPS):
        if group == 0:
            wait_all(copies[PLANES:])
        wait_all(copies[first : first + count])
        for plane in range(first, first + count):
            hit = (first_plane + plane == cell_ref[member, 0]).astype(jnp.float32)
            values = jnp.concatenate([w_ref[plane, 0] + hit * impulse, w_ref[plane, 1]], axis=1)
            values = dot(three_terms(values, 1), z_ref[...])
            real, imag = long_transform(y_ref[...], values, 1)
            out_ref[:, :, plane, 0] = real.reshape(ZL, QUADS, KY, NZ)
            out_ref[:, :, plane, 1] = imag.reshape(ZL, QUADS, KY, NZ)
        part = pl.ds(first, count)
        outs += start_all(
            [(out_ref.at[:, :, part], out_hbm.at[:, :, part])], out_sem.at[pl.ds(group, 1)]
        )
    wait_all(outs)


def forward(source, member, cells, z_dft, y_dft):
    shape = (ZL, QUADS, PLANES, 2, KY, NZ)
    return kernel_call(
        functools.partial(forward_kernel, member),
        "forward_zy",
        (cells, source, z_dft, y_dft),
        [shape],
        [
            pltpu.VMEM((PLANES, 2, NY, NZ), jnp.float32),
            *table_scratch(z_dft, y_dft),
            pltpu.VMEM(shape, jnp.float32),
            pltpu.SemaphoreType.DMA((PLANES + 2,)),
            pltpu.SemaphoreType.DMA((len(GROUPS),)),
        ],
        FLOPS,
        5 * 2**20,
        smem=1,
    )[0].reshape(PARTS, PLANES, 2, KY, NZ)


def spectral_kernel(chunks, forms, n_in, n_all, *refs):
    in_hbm, (green_hbm, x_hbm, back_hbm) = refs[:n_in], refs[n_in : n_in + 3]
    refs = refs[n_all:]
    n_out = sum(QUADS if form == PARTNERS else 1 for form in forms)
    out_hbm, refs = refs[:n_out], refs[n_out:]
    in_ref, green_ref, x_ref, back_ref, *out_refs, sem, out_sem = refs
    others = start_all([(x_hbm, x_ref), (green_hbm, green_ref), (back_hbm, back_ref)], sem)
    here = lax.axis_index(PENCIL)
    *slots, whole = in_hbm
    early = slots[0].shape[1] if slots else 0
    pairs = [(whole, in_ref.at[:, pl.ds(early, PLANES - early)])]
    for a, slot in enumerate(slots):
        for j in range(QUADS):
            pairs.append((slot.at[j], in_ref.at[here ^ (a * QUADS + j), pl.ds(0, early)]))
    inputs = start_all(pairs, sem.at[pl.ds(3, len(pairs))])
    flat = [ref.reshape(PARTS * chunk * 2 * KY, NZ) for ref, chunk in zip(out_refs, chunks)]
    flat_in = in_ref.reshape(PARTS * PLANES * 2 * KY, NZ)
    wait_all([others[0], *inputs])

    def take(c, ky):
        return flat_in[pl.ds(c * KY + ky, NX, stride=2 * KY), :]

    for ky in range(KY):
        values = jnp.concatenate([take(c, ky) for c in range(2)], axis=1)
        real, imag = long_transform(x_ref[...], values, 1)
        if ky == 0:
            wait_all(others[1:])
        green_re = green_ref[pl.ds(ky, NX, stride=KY), :]
        green_im = green_ref[pl.ds(NX * KY + ky, NX, stride=KY), :]
        values = jnp.concatenate(
            [green_re * real - green_im * imag, green_re * imag + green_im * real], axis=1
        )
        results = long_transform(back_ref[...], values, -1)
        at = 0
        for chunk, out_ref in zip(chunks, flat):
            for plane in range(chunk):
                for c in range(2):
                    first = (plane * 2 + c) * KY + ky
                    out_ref[pl.ds(first, PARTS, stride=chunk * 2 * KY), :] = results[c][at : at + PARTS]
                at += PARTS
    pairs, at = [], 0
    for form, ref in zip(forms, out_refs):
        if form == PARTNERS:
            pairs += [(ref.at[:, quad_of(j)], out_hbm[at + j]) for j in range(QUADS)]
            at += QUADS
        else:
            target = out_hbm[at]
            pairs.append((ref, target if form == WHOLE else target.at[:, :, form]))
            at += 1
    wait_all(start_all(pairs, out_sem))


def spectral(spectra, green, chunks, forms, x_dft, back_dft, earlier=()):
    operands = (*spectra, green.reshape(2 * NX * KY, NZ), x_dft, back_dft, *earlier)
    shapes, aliases = [], {}
    for form, chunk in zip(forms, chunks):
        tail = (chunk, 2, KY, NZ)
        if form == PARTNERS:
            shapes += [(ZL, *tail)] * QUADS
        elif form == WHOLE:
            shapes.append((ZL, QUADS, *tail))
        else:
            if earlier:
                aliases[len(operands) - 1] = len(shapes)
            shapes.append((ZL, QUADS, 2, *tail))
    return kernel_call(
        functools.partial(spectral_kernel, chunks, forms, len(spectra), len(operands)),
        "spectral",
        operands,
        shapes,
        [
            pltpu.VMEM((PARTS, PLANES, 2, KY, NZ), jnp.float32),
            pltpu.VMEM((2 * NX * KY, NZ), jnp.float32),
            *table_scratch(x_dft, back_dft),
            *[pltpu.VMEM((ZL, QUADS, chunk, 2, KY, NZ), jnp.float32) for chunk in chunks],
            pltpu.SemaphoreType.DMA((4 + (PARTS if len(spectra) > 1 else 0),)),
            pltpu.SemaphoreType.DMA((len(shapes),)),
        ],
        FLOPS,
        8 * 2**20,
        aliases=aliases,
    )


def pack_kernel(*refs):
    arrived, packed = refs[:QUADS], refs[QUADS : QUADS + ZL]
    held, sem, out_sem = refs[QUADS + ZL :]
    here = lax.axis_index("zl")
    wait_all(start_all([(ref, held.at[j]) for j, ref in enumerate(arrived)], sem))
    wait_all(start_all([(held.at[:, here ^ a], out) for a, out in enumerate(packed)], out_sem))


def over_quads(values):
    arrived = [
        values[0],
        *[
            lax.ppermute(values[j], ("x", "core"), [(i, i ^ j) for i in range(QUADS)])
            for j in range(1, QUADS)
        ],
    ]
    return kernel_call(
        pack_kernel,
        "pack",
        tuple(arrived),
        [(QUADS, *values[0].shape[1:])] * ZL,
        [
            pltpu.VMEM((QUADS, *values[0].shape), jnp.float32),
            pltpu.SemaphoreType.DMA((QUADS,)),
            pltpu.SemaphoreType.DMA((ZL,)),
        ],
        0,
        4 * 2**20,
    )


def over_z(values):
    return [
        values[0],
        *[
            lax.ppermute(values[a], "zl", [(i, i ^ a) for i in range(ZL)])
            for a in range(1, ZL)
        ],
    ]


def inverse_kernel(inside, start, count, n_in, *refs):
    f_hbm, refs = refs[:n_in], refs[n_in:]
    w_hbm, z_hbm, y_hbm, u_hbm, *refs = refs
    sum_hbm = refs[:YY]
    f_ref, w_ref, z_ref, y_ref, u_ref, sum_ref, sem, out_sem = refs[YY:]
    here = lax.axis_index("y")
    slots = [lax.axis_index(PENCIL) ^ part for part in range(PARTS)]
    tables = start_all([(y_hbm, y_ref), (z_hbm, z_ref)], sem)
    part = pl.ds(inside, count)
    if n_in == 1:
        pairs = [(f_hbm[0].at[:, member, part], f_ref.at[member]) for member in range(2)]
    else:
        pairs = [
            (f_hbm[a].at[:, part], f_ref.at[0, pl.ds(a * QUADS, QUADS)]) for a in range(ZL)
        ]
        pairs.append((f_hbm[ZL].at[:, part], f_ref.at[1]))
    inputs = start_all(pairs, sem.at[pl.ds(2, len(pairs))])
    sources = start_all(
        [(w_hbm.at[:, :, start + plane], w_ref.at[plane]) for plane in range(count)],
        sem.at[pl.ds(3 + ZL, count)],
    )
    wait_all([*tables, *inputs])
    for plane in range(count):
        for member in range(2):
            values = jnp.concatenate(
                [
                    f_ref[member, :, plane, c].reshape(NY, NZ)
                    if member == 1 or n_in == 1
                    else jnp.concatenate([f_ref[0, slot, plane, c] for slot in slots], axis=0)
                    for c in range(2)
                ],
                axis=1,
            )
            real, imag = long_transform(y_ref[...], values, -1)
            field = dot(three_terms(jnp.concatenate([real, imag], axis=1), 1), z_ref[...])
            u_ref[plane, member, 0] = field[:, :NZ]
            u_ref[plane, member, 1] = field[:, NZ:]
    outs = start_all([(u_ref, u_hbm)], out_sem.at[pl.ds(YY, 1)])
    wait_all(sources)
    for plane in range(count):
        for h in range(ZH):
            for y in range(YY):
                rows = pl.ds((h * YY + y) * SHARE, SHARE)
                totals = None
                for member in range(2):
                    real, imag = u_ref[plane, member, 0, rows], u_ref[plane, member, 1, rows]
                    source_re, source_im = w_ref[plane, member, 0, rows], w_ref[plane, member, 1, rows]
                    terms = (
                        real * source_re + imag * source_im,
                        real * source_im - imag * source_re,
                        real * real + imag * imag,
                    )
                    totals = terms if totals is None else [a + b for a, b in zip(totals, terms)]
                for kind in range(3):
                    sum_ref[y, h, kind, plane] = totals[kind]
    outs += start_all(
        [(sum_ref.at[lax.rem(here + shift, YY)], sum_hbm[shift]) for shift in range(YY)], out_sem
    )
    wait_all(outs)


def inverse(fields, sources, inside, start, count, z_dft, y_dft):
    sum_shape = (ZH, 3, count, SHARE, NZ)
    u_shape = (count, 2, 2, NY, NZ)
    outs = kernel_call(
        functools.partial(inverse_kernel, inside, start, count, len(fields)),
        "inverse_yz",
        (*fields, sources, z_dft, y_dft),
        [u_shape, *[sum_shape] * YY],
        [
            pltpu.VMEM((2, PARTS, count, 2, KY, NZ), jnp.float32),
            pltpu.VMEM(u_shape, jnp.float32),
            *table_scratch(z_dft, y_dft),
            pltpu.VMEM(u_shape, jnp.float32),
            pltpu.VMEM((YY, *sum_shape), jnp.float32),
            pltpu.SemaphoreType.DMA((3 + ZL + count,)),
            pltpu.SemaphoreType.DMA((YY + 1,)),
        ],
        FLOPS,
        4 * 2**20 * count // 2,
    )
    return outs[0], outs[1:]


def update_kernel(start, count, *refs):
    *refs, u_ref, w_ref, part_ref, new_ref, sem, out_sem = refs
    parts, u_hbm, w_hbm, out_hbm = refs[:YY], refs[YY], refs[YY + 1], refs[-1]
    here = lax.axis_index("y")
    planes = pl.ds(start, count)
    wait_all(
        start_all(
            [
                (w_hbm.at[:, :, planes], w_ref),
                (u_hbm, u_ref),
                *[(part, part_ref.at[shift]) for shift, part in enumerate(parts)],
            ],
            sem,
        )
    )
    outs = []
    for plane in range(count):
        for shift in range(YY):
            y = lax.rem(here + YY - shift, YY)
            for h in range(ZH):
                rows = pl.ds(pl.multiple_of((h * YY + y) * SHARE, SHARE), SHARE)
                real, imag = part_ref[shift, h, 0, plane], part_ref[shift, h, 1, plane]
                for member in range(2):
                    field_re, field_im = u_ref[plane, member, 0, rows], u_ref[plane, member, 1, rows]
                    scatter_re = real * field_re - imag * field_im
                    scatter_im = real * field_im + imag * field_re
                    new_ref[member, 0, plane, rows] = 0.5 * (w_ref[member, 0, plane, rows] + scatter_re)
                    new_ref[member, 1, plane, rows] = 0.5 * (w_ref[member, 1, plane, rows] + scatter_im)
        outs += start_all(
            [(new_ref.at[:, :, plane], out_hbm.at[:, :, start + plane])], out_sem.at[pl.ds(plane, 1)]
        )
    wait_all(outs)


def update(parts, fields, sources, start, count, earlier):
    more = () if earlier is None else (earlier,)
    block = (2, 2, count, NY, NZ)
    return kernel_call(
        functools.partial(update_kernel, start, count),
        "update",
        (*parts, fields, sources, *more),
        [sources.shape],
        [
            pltpu.VMEM(fields.shape, jnp.float32),
            pltpu.VMEM(block, jnp.float32),
            pltpu.VMEM((YY, ZH, 2, count, SHARE, NZ), jnp.float32),
            pltpu.VMEM(block, jnp.float32),
            pltpu.SemaphoreType.DMA((2 + YY,)),
            pltpu.SemaphoreType.DMA((count,)),
        ],
        FLOPS,
        1800 * 1024 * count,
        aliases={YY + 2: 0} if more else None,
    )[0]


def exchange(values):
    return lax.all_to_all(values, PENCIL, split_axis=0, concat_axis=0, tiled=True)


def along_y(values, shift):
    return lax.ppermute(values, "y", [(i, (i + shift) % YY) for i in range(YY)])


def reduce_y(sums):
    arrived = [along_y(sums[shift], shift) for shift in range(1, YY)]
    return sums[0] + arrived[0] + arrived[1] + arrived[2]


def contrast_of(mine, earlier):
    other = lax.ppermute(mine, "zh", [(0, 1), (1, 0)])
    both = mine + (after(other, earlier) if earlier else other)
    return both[:, :2] / (1.0 + both[:, 2:])


def share_contrast(contrast):
    return [contrast, *[along_y(contrast, shift) for shift in range(1, YY)]]


CHUNKS = (4, 4)
PIECES = ((2, 2), (2, 2))


def after(values, others):
    return lax.optimization_barrier((values, others))[0]


def shards(contrast_source, green_spectrum, source_cells):
    order = np.arange(NX).reshape(PARTS, PLANES).T.reshape(-1)
    y_dft = jnp.asarray(long_table())
    back_dft = jnp.asarray(long_table(order))
    z_forward = jnp.asarray(z_table(1))
    z_back = jnp.asarray(z_table(-1))

    spectra = [
        exchange(forward(contrast_source, member, source_cells, z_forward, y_dft))
        for member in range(2)
    ]
    *early, both = spectral(
        [spectra[0]], green_spectrum, CHUNKS, (PARTNERS, 0), y_dft, back_dft
    )
    early = over_quads(early)
    whole = after(spectra[1], early)
    early = over_z(early)
    single, both = spectral(
        [whole], green_spectrum, CHUNKS, (WHOLE, 1), y_dft, back_dft, (both,)
    )
    single = exchange(after(single, early).reshape(PARTS, CHUNKS[0], 2, KY, NZ))
    both = exchange(both.reshape(PARTS, 2, CHUNKS[1], 2, KY, NZ))

    def part_of(fields, inside, start, count, before_sums, before_contrast):
        field, sums = inverse(fields, contrast_source, inside, start, count, z_back, y_dft)
        mine, before_sums = lax.optimization_barrier((reduce_y(sums), before_sums))
        contrast = contrast_of(mine, before_contrast)
        share = lax.dynamic_index_in_dim(contrast, lax.axis_index("zh"), 0, keepdims=False)
        return share, (share_contrast(contrast), field), before_sums

    def renew(pair, start, count, updated):
        return update(*pair, contrast_source, start, count, updated)

    (a1, a2), (b1, b2) = PIECES
    first, second = (*early, single), (both,)
    share_a1, pair_a1, _ = part_of(first, 0, 0, a1, (), None)
    share_a2, pair_a2, _ = part_of(first, a1, a1, a2, (), None)
    updated = renew(pair_a1, 0, a1, None)
    second, updated, pair_a2 = lax.optimization_barrier((second, updated, pair_a2))
    share_b1, pair_b1, _ = part_of(second, 0, a1 + a2, b1, (), None)
    share_b2, pair_b2, pair_a2 = part_of(second, b1, a1 + a2 + b1, b2, pair_a2, pair_b1[0])
    updated = renew(pair_a2, a1, a2, updated)
    updated = renew(pair_b1, a1 + a2, b1, updated)
    updated = renew(pair_b2, a1 + a2 + b1, b2, updated)
    return updated, jnp.concatenate([share_a1, share_a2, share_b1, share_b2], axis=1)


def solution(mesh):
    fine = Mesh(mesh.devices.reshape(ZH, YY, 4, 4, 2), (*SHOT, *PENCIL))
    return jax.shard_map(
        shards,
        mesh=fine,
        in_specs=(
            P(SHOT, None, PENCIL, None, None),
            P(None, None, PENCIL, None),
            P(SHOT, None),
        ),
        out_specs=(P(SHOT, None, PENCIL, None, None), P(None, PENCIL, SHOT, None)),
        check_vma=False,
    )
```

```python
import functools
import math

import jax
import jax.numpy as jnp
import ml_dtypes
import numpy as np
from jax import lax
from jax.experimental import pallas as pl
from jax.experimental.pallas import tpu as pltpu
from jax.sharding import Mesh, PartitionSpec as P

SHOT = ("zh", "y")
PENCIL = ("zl", "x", "core")
ZH, YY = 2, 4
ZL, QUADS = 4, 8
PARTS = ZL * QUADS
NX, NY, NZ = 256, 256, 128
PLANES = NX // PARTS
KY = NY // PARTS
SHARE = NY // (ZH * YY)
GROUPS = ((0, 2), (2, 4), (6, 2))
FLOPS = 10**6
PARTNERS, WHOLE = -1, -2
VMEM_LIMIT = 62 * 1024 * 1024


def split_table(table):
    high = table.astype(ml_dtypes.bfloat16)
    return high, (table - high.astype(np.float64)).astype(ml_dtypes.bfloat16)


def cos_sin(length):
    index = np.arange(length)
    angle = 2.0 * np.pi * (index[:, None] * index[None, :] % length) / length
    return np.cos(angle) / math.sqrt(length), np.sin(angle) / math.sqrt(length)


def long_table():
    cosine, sine = cos_sin(NY)
    high, low = split_table(np.concatenate([cosine, sine], axis=0))
    return np.concatenate([high, high, low], axis=1)


def z_table(sign):
    cosine, sine = cos_sin(NZ)
    high, low = split_table(np.block([[cosine, -sign * sine], [sign * sine, cosine]]))
    return np.concatenate([high, high, low], axis=0)


def three_terms(values, axis):
    high = values.astype(jnp.bfloat16)
    low = (values - high.astype(jnp.float32)).astype(jnp.bfloat16)
    return jnp.concatenate([high, low, high], axis=axis)


def dot(left, right):
    return lax.dot_general(left, right, (((1,), (0,)), ((), ())), preferred_element_type=jnp.float32)


def long_transform(table, values, sign):
    both = dot(table, three_terms(values, 0))
    count, lanes = both.shape[0] // 2, both.shape[1] // 2
    cos_re, cos_im = both[:count, :lanes], both[:count, lanes:]
    sin_re, sin_im = both[count:, :lanes], both[count:, lanes:]
    if sign > 0:
        return cos_re + sin_im, cos_im - sin_re
    return cos_re - sin_im, cos_im + sin_re


ANY = pl.BlockSpec(memory_space=pl.ANY)


def quad_of(j):
    return lax.axis_index(("x", "core")) ^ j


def kernel_call(body, name, operands, out_shapes, scratch, flops, nbytes, aliases=None, smem=0):
    return pl.pallas_call(
        body,
        in_specs=[
            *[pl.BlockSpec(memory_space=pltpu.SMEM)] * smem,
            *[ANY] * (len(operands) - smem),
        ],
        out_specs=[ANY] * len(out_shapes),
        out_shape=[jax.ShapeDtypeStruct(shape, jnp.float32) for shape in out_shapes],
        scratch_shapes=scratch,
        input_output_aliases=aliases or {},
        compiler_params=pltpu.CompilerParams(vmem_limit_bytes=VMEM_LIMIT),
        cost_estimate=pl.CostEstimate(flops=flops, bytes_accessed=nbytes, transcendentals=0),
        name=name,
    )(*operands)


def table_scratch(*tables):
    return [pltpu.VMEM(t.shape, t.dtype) for t in tables]


def start_all(pairs, semaphores):
    copies = [
        pltpu.make_async_copy(source, target, semaphores.at[i])
        for i, (source, target) in enumerate(pairs)
    ]
    for copy in copies:
        copy.start()
    return copies


def wait_all(copies):
    for copy in copies:
        copy.wait()


def forward_kernel(
    member, cell_ref, w_hbm, z_hbm, y_hbm, out_hbm, w_ref, z_ref, y_ref, out_ref, sem, out_sem
):
    pairs = [(w_hbm.at[member, :, plane], w_ref.at[plane]) for plane in range(PLANES)]
    tables = start_all([(z_hbm, z_ref), (y_hbm, y_ref)], sem.at[pl.ds(PLANES, 2)])
    copies = [*start_all(pairs, sem.at[pl.ds(0, PLANES)]), *tables]
    first_plane = lax.axis_index(PENCIL) * PLANES
    row = lax.broadcasted_iota(jnp.int32, (NY, NZ), 0)
    column = lax.broadcasted_iota(jnp.int32, (NY, NZ), 1)
    here = (row == cell_ref[member, 1]) & (column == cell_ref[member, 2])
    impulse = jnp.where(here, math.sqrt(NX * NY * NZ), 0.0)
    outs = []
    for group, (first, count) in enumerate(GROUPS):
        if group == 0:
            wait_all(copies[PLANES:])
        wait_all(copies[first : first + count])
        for plane in range(first, first + count):
            hit = (first_plane + plane == cell_ref[member, 0]).astype(jnp.float32)
            values = jnp.concatenate([w_ref[plane, 0] + hit * impulse, w_ref[plane, 1]], axis=1)
            values = dot(three_terms(values, 1), z_ref[...])
            real, imag = long_transform(y_ref[...], values, 1)
            out_ref[:, :, plane, 0] = real.reshape(ZL, QUADS, KY, NZ)
            out_ref[:, :, plane, 1] = imag.reshape(ZL, QUADS, KY, NZ)
        part = pl.ds(first, count)
        outs += start_all(
            [(out_ref.at[:, :, part], out_hbm.at[:, :, part])], out_sem.at[pl.ds(group, 1)]
        )
    wait_all(outs)


def forward(source, member, cells, z_dft, y_dft):
    shape = (ZL, QUADS, PLANES, 2, KY, NZ)
    return kernel_call(
        functools.partial(forward_kernel, member),
        "forward_zy",
        (cells, source, z_dft, y_dft),
        [shape],
        [
            pltpu.VMEM((PLANES, 2, NY, NZ), jnp.float32),
            *table_scratch(z_dft, y_dft),
            pltpu.VMEM(shape, jnp.float32),
            pltpu.SemaphoreType.DMA((PLANES + 2,)),
            pltpu.SemaphoreType.DMA((len(GROUPS),)),
        ],
        FLOPS,
        5 * 2**20,
        smem=1,
    )[0].reshape(PARTS, PLANES, 2, KY, NZ)


def spectral_kernel(chunks, forms, n_in, n_all, *refs):
    in_hbm, (green_hbm, x_hbm) = refs[:n_in], refs[n_in : n_in + 2]
    refs = refs[n_all:]
    n_out = sum(QUADS if form == PARTNERS else 1 for form in forms)
    out_hbm, refs = refs[:n_out], refs[n_out:]
    in_ref, green_ref, x_ref, out_ref, sem, out_sem = refs
    others = start_all([(x_hbm, x_ref), (green_hbm, green_ref)], sem)
    here = lax.axis_index(PENCIL)
    *slots, whole = in_hbm
    early = slots[0].shape[1] if slots else 0
    pairs = [(whole, in_ref.at[:, pl.ds(early, PLANES - early)])]
    for a, slot in enumerate(slots):
        for j in range(QUADS):
            pairs.append((slot.at[j], in_ref.at[here ^ (a * QUADS + j), pl.ds(0, early)]))
    inputs = start_all(pairs, sem.at[pl.ds(3, len(pairs))])
    flat = out_ref.reshape(PARTS * PLANES * 2 * KY, NZ)
    flat_in = in_ref.reshape(PARTS * PLANES * 2 * KY, NZ)
    wait_all([others[0], *inputs])

    def take(c, ky):
        return flat_in[pl.ds(c * KY + ky, NX, stride=2 * KY), :]

    for ky in range(KY):
        values = jnp.concatenate([take(c, ky) for c in range(2)], axis=1)
        real, imag = long_transform(x_ref[...], values, 1)
        if ky == 0:
            wait_all(others[1:])
        green_re = green_ref[pl.ds(ky, NX, stride=KY), :]
        green_im = green_ref[pl.ds(NX * KY + ky, NX, stride=KY), :]
        values = jnp.concatenate(
            [green_re * real - green_im * imag, green_re * imag + green_im * real], axis=1
        )
        results = long_transform(x_ref[...], values, -1)
        for c in range(2):
            flat[pl.ds(c * KY + ky, NX, stride=2 * KY), :] = results[c]
    pairs, at, first = [], 0, 0
    for form, chunk in zip(forms, chunks):
        ref = out_ref.at[:, :, pl.ds(first, chunk)]
        first += chunk
        if form == PARTNERS:
            pairs += [
                (out_ref.at[:, quad_of(j), pl.ds(first - chunk, chunk)], out_hbm[at + j])
                for j in range(QUADS)
            ]
            at += QUADS
        else:
            target = out_hbm[at]
            pairs.append((ref, target if form == WHOLE else target.at[:, :, form]))
            at += 1
    wait_all(start_all(pairs, out_sem))


def spectral(spectra, green, chunks, forms, x_dft, earlier=()):
    operands = (*spectra, green.reshape(2 * NX * KY, NZ), x_dft, *earlier)
    shapes, aliases = [], {}
    for form, chunk in zip(forms, chunks):
        tail = (chunk, 2, KY, NZ)
        if form == PARTNERS:
            shapes += [(ZL, *tail)] * QUADS
        elif form == WHOLE:
            shapes.append((ZL, QUADS, *tail))
        else:
            if earlier:
                aliases[len(operands) - 1] = len(shapes)
            shapes.append((ZL, QUADS, 2, *tail))
    return kernel_call(
        functools.partial(spectral_kernel, chunks, forms, len(spectra), len(operands)),
        "spectral",
        operands,
        shapes,
        [
            pltpu.VMEM((PARTS, PLANES, 2, KY, NZ), jnp.float32),
            pltpu.VMEM((2 * NX * KY, NZ), jnp.float32),
            *table_scratch(x_dft),
            pltpu.VMEM((ZL, QUADS, PLANES, 2, KY, NZ), jnp.float32),
            pltpu.SemaphoreType.DMA((4 + (PARTS if len(spectra) > 1 else 0),)),
            pltpu.SemaphoreType.DMA((len(shapes),)),
        ],
        FLOPS,
        8 * 2**20,
        aliases=aliases,
    )


def pack_kernel(*refs):
    arrived, packed = refs[:QUADS], refs[QUADS : QUADS + ZL]
    held, sem, out_sem = refs[QUADS + ZL :]
    here = lax.axis_index("zl")
    wait_all(start_all([(ref, held.at[j]) for j, ref in enumerate(arrived)], sem))
    wait_all(start_all([(held.at[:, here ^ a], out) for a, out in enumerate(packed)], out_sem))


def over_quads(values):
    arrived = [
        values[0],
        *[
            lax.ppermute(values[j], ("x", "core"), [(i, i ^ j) for i in range(QUADS)])
            for j in range(1, QUADS)
        ],
    ]
    return kernel_call(
        pack_kernel,
        "pack",
        tuple(arrived),
        [(QUADS, *values[0].shape[1:])] * ZL,
        [
            pltpu.VMEM((QUADS, *values[0].shape), jnp.float32),
            pltpu.SemaphoreType.DMA((QUADS,)),
            pltpu.SemaphoreType.DMA((ZL,)),
        ],
        0,
        4 * 2**20,
    )


def over_z(values):
    return [
        values[0],
        *[
            lax.ppermute(values[a], "zl", [(i, i ^ a) for i in range(ZL)])
            for a in range(1, ZL)
        ],
    ]


def inverse_kernel(inside, start, count, n_in, *refs):
    f_hbm, refs = refs[:n_in], refs[n_in:]
    w_hbm, z_hbm, y_hbm, u_hbm, *refs = refs
    sum_hbm = refs[:YY]
    f_ref, w_ref, z_ref, y_ref, u_ref, sum_ref, sem, out_sem = refs[YY:]
    here = lax.axis_index("y")
    slots = [lax.axis_index(PENCIL) ^ part for part in range(PARTS)]
    tables = start_all([(y_hbm, y_ref), (z_hbm, z_ref)], sem)
    part = pl.ds(inside, count)
    if n_in == 1:
        pairs = [(f_hbm[0].at[:, member, part], f_ref.at[member]) for member in range(2)]
    else:
        pairs = [
            (f_hbm[a].at[:, part], f_ref.at[0, pl.ds(a * QUADS, QUADS)]) for a in range(ZL)
        ]
        pairs.append((f_hbm[ZL].at[:, part], f_ref.at[1]))
    inputs = start_all(pairs, sem.at[pl.ds(2, len(pairs))])
    sources = start_all(
        [(w_hbm.at[:, :, start + plane], w_ref.at[plane]) for plane in range(count)],
        sem.at[pl.ds(3 + ZL, count)],
    )
    wait_all([*tables, *inputs])
    for plane in range(count):
        for member in range(2):
            values = jnp.concatenate(
                [
                    f_ref[member, :, plane, c].reshape(NY, NZ)
                    if member == 1 or n_in == 1
                    else jnp.concatenate([f_ref[0, slot, plane, c] for slot in slots], axis=0)
                    for c in range(2)
                ],
                axis=1,
            )
            real, imag = long_transform(y_ref[...], values, -1)
            field = dot(three_terms(jnp.concatenate([real, imag], axis=1), 1), z_ref[...])
            u_ref[plane, member, 0] = field[:, :NZ]
            u_ref[plane, member, 1] = field[:, NZ:]
    outs = start_all([(u_ref, u_hbm)], out_sem.at[pl.ds(YY, 1)])
    wait_all(sources)
    for plane in range(count):
        for h in range(ZH):
            for y in range(YY):
                rows = pl.ds((h * YY + y) * SHARE, SHARE)
                totals = None
                for member in range(2):
                    real, imag = u_ref[plane, member, 0, rows], u_ref[plane, member, 1, rows]
                    source_re, source_im = w_ref[plane, member, 0, rows], w_ref[plane, member, 1, rows]
                    terms = (
                        real * source_re + imag * source_im,
                        real * source_im - imag * source_re,
                        real * real + imag * imag,
                    )
                    totals = terms if totals is None else [a + b for a, b in zip(totals, terms)]
                for kind in range(3):
                    sum_ref[y, h, kind, plane] = totals[kind]
    outs += start_all(
        [(sum_ref.at[lax.rem(here + shift, YY)], sum_hbm[shift]) for shift in range(YY)], out_sem
    )
    wait_all(outs)


def inverse(fields, sources, inside, start, count, z_dft, y_dft):
    sum_shape = (ZH, 3, count, SHARE, NZ)
    u_shape = (count, 2, 2, NY, NZ)
    outs = kernel_call(
        functools.partial(inverse_kernel, inside, start, count, len(fields)),
        "inverse_yz",
        (*fields, sources, z_dft, y_dft),
        [u_shape, *[sum_shape] * YY],
        [
            pltpu.VMEM((2, PARTS, count, 2, KY, NZ), jnp.float32),
            pltpu.VMEM(u_shape, jnp.float32),
            *table_scratch(z_dft, y_dft),
            pltpu.VMEM(u_shape, jnp.float32),
            pltpu.VMEM((YY, *sum_shape), jnp.float32),
            pltpu.SemaphoreType.DMA((3 + ZL + count,)),
            pltpu.SemaphoreType.DMA((YY + 1,)),
        ],
        FLOPS,
        4 * 2**20 * count // 2,
    )
    return outs[0], outs[1:]


def update_kernel(start, count, *refs):
    *refs, u_ref, w_ref, part_ref, new_ref, sem, out_sem = refs
    parts, u_hbm, w_hbm, out_hbm = refs[:YY], refs[YY], refs[YY + 1], refs[-1]
    here = lax.axis_index("y")
    planes = pl.ds(start, count)
    wait_all(
        start_all(
            [
                (w_hbm.at[:, :, planes], w_ref),
                (u_hbm, u_ref),
                *[(part, part_ref.at[shift]) for shift, part in enumerate(parts)],
            ],
            sem,
        )
    )
    outs = []
    for plane in range(count):
        for shift in range(YY):
            y = lax.rem(here + YY - shift, YY)
            for h in range(ZH):
                rows = pl.ds(pl.multiple_of((h * YY + y) * SHARE, SHARE), SHARE)
                real, imag = part_ref[shift, h, 0, plane], part_ref[shift, h, 1, plane]
                for member in range(2):
                    field_re, field_im = u_ref[plane, member, 0, rows], u_ref[plane, member, 1, rows]
                    scatter_re = real * field_re - imag * field_im
                    scatter_im = real * field_im + imag * field_re
                    new_ref[member, 0, plane, rows] = 0.5 * (w_ref[member, 0, plane, rows] + scatter_re)
                    new_ref[member, 1, plane, rows] = 0.5 * (w_ref[member, 1, plane, rows] + scatter_im)
        outs += start_all(
            [(new_ref.at[:, :, plane], out_hbm.at[:, :, start + plane])], out_sem.at[pl.ds(plane, 1)]
        )
    wait_all(outs)


def update(parts, fields, sources, start, count, earlier):
    more = () if earlier is None else (earlier,)
    block = (2, 2, count, NY, NZ)
    return kernel_call(
        functools.partial(update_kernel, start, count),
        "update",
        (*parts, fields, sources, *more),
        [sources.shape],
        [
            pltpu.VMEM(fields.shape, jnp.float32),
            pltpu.VMEM(block, jnp.float32),
            pltpu.VMEM((YY, ZH, 2, count, SHARE, NZ), jnp.float32),
            pltpu.VMEM(block, jnp.float32),
            pltpu.SemaphoreType.DMA((2 + YY,)),
            pltpu.SemaphoreType.DMA((count,)),
        ],
        FLOPS,
        1800 * 1024 * count,
        aliases={YY + 2: 0} if more else None,
    )[0]


def exchange(values):
    return lax.all_to_all(values, PENCIL, split_axis=0, concat_axis=0, tiled=True)


def along_y(values, shift):
    return lax.ppermute(values, "y", [(i, (i + shift) % YY) for i in range(YY)])


def reduce_y(sums):
    arrived = [along_y(sums[shift], shift) for shift in range(1, YY)]
    return sums[0] + arrived[0] + arrived[1] + arrived[2]


def contrast_of(mine, earlier):
    other = lax.ppermute(mine, "zh", [(0, 1), (1, 0)])
    both = mine + (after(other, earlier) if earlier else other)
    return both[:, :2] / (1.0 + both[:, 2:])


def share_contrast(contrast):
    return [contrast, *[along_y(contrast, shift) for shift in range(1, YY)]]


CHUNKS = (4, 4)
PIECES = ((2, 2), (2, 2))


def after(values, others):
    return lax.optimization_barrier((values, others))[0]


def shards(contrast_source, green_spectrum, source_cells):
    y_dft = jnp.asarray(long_table())
    z_forward = jnp.asarray(z_table(1))
    z_back = jnp.asarray(z_table(-1))

    spectra = [
        exchange(forward(contrast_source, member, source_cells, z_forward, y_dft))
        for member in range(2)
    ]
    *early, both = spectral(
        [spectra[0]], green_spectrum, CHUNKS, (PARTNERS, 0), y_dft
    )
    early = over_quads(early)
    whole = after(spectra[1], early)
    early = over_z(early)
    single, both = spectral(
        [whole], green_spectrum, CHUNKS, (WHOLE, 1), y_dft, (both,)
    )
    single = exchange(after(single, early).reshape(PARTS, CHUNKS[0], 2, KY, NZ))
    both = exchange(both.reshape(PARTS, 2, CHUNKS[1], 2, KY, NZ))

    def part_of(fields, inside, start, count, before_sums, before_contrast):
        field, sums = inverse(fields, contrast_source, inside, start, count, z_back, y_dft)
        mine, before_sums = lax.optimization_barrier((reduce_y(sums), before_sums))
        contrast = contrast_of(mine, before_contrast)
        share = lax.dynamic_index_in_dim(contrast, lax.axis_index("zh"), 0, keepdims=False)
        return share, (share_contrast(contrast), field), before_sums

    def renew(pair, start, count, updated):
        return update(*pair, contrast_source, start, count, updated)

    (a1, a2), (b1, b2) = PIECES
    first, second = (*early, single), (both,)
    share_a1, pair_a1, _ = part_of(first, 0, 0, a1, (), None)
    share_a2, pair_a2, _ = part_of(first, a1, a1, a2, (), None)
    updated = renew(pair_a1, 0, a1, None)
    second, updated, pair_a2 = lax.optimization_barrier((second, updated, pair_a2))
    share_b1, pair_b1, _ = part_of(second, 0, a1 + a2, b1, (), None)
    share_b2, pair_b2, pair_a2 = part_of(second, b1, a1 + a2 + b1, b2, pair_a2, pair_b1[0])
    updated = renew(pair_a2, a1, a2, updated)
    updated = renew(pair_b1, a1 + a2, b1, updated)
    updated = renew(pair_b2, a1 + a2 + b1, b2, updated)
    return updated, jnp.concatenate([share_a1, share_a2, share_b1, share_b2], axis=1)


def solution(mesh):
    fine = Mesh(mesh.devices.reshape(ZH, YY, 4, 4, 2), (*SHOT, *PENCIL))
    return jax.shard_map(
        shards,
        mesh=fine,
        in_specs=(
            P(SHOT, None, PENCIL, None, None),
            P(None, None, PENCIL, None),
            P(SHOT, None),
        ),
        out_specs=(P(SHOT, None, PENCIL, None, None), P(None, PENCIL, SHOT, None)),
        check_vma=False,
    )
```
